32 devices in a mesh: member: 2 (over y), lon: 16 (over z, x, core).
Axes of the slice: x: 2, y: 2, z: 4, core: 2. Of those that a mesh axis runs over, the one named last changes fastest.
Arguments:
- state_start: float32 [190, 256, 128], P('member', 'lon'), parts along dimension 0, may hold values from -6 to 6
- lift_weight: bfloat16 [95, 256], replicated, may hold values from -0.625 to 0.625
- conv_kernel: float32 [49, 256], replicated, may hold values from -0.875 to 0.875
- norm_gain: float32 [256], replicated, may hold values from 0.1 to 1.9
- up_weight: bfloat16 [256, 1024], replicated, may hold values from -0.375 to 0.375
- down_weight: bfloat16 [1024, 256], replicated, may hold values from -0.1875 to 0.1875
- out_weight: bfloat16 [256, 95], replicated, may hold values from -0.375 to 0.375
- obs_cells: int32 [4, 256, 32, 4], P('member', 'lon'), parts along dimension 0, may hold values from 0 to 127
- obs_weights: float32 [4, 256, 32, 4], P('member', 'lon'), parts along dimension 0, may hold values from 0.1 to 1
- tile_counts: int32 [4, 256], P('member', 'lon'), parts along dimension 0, may hold values from 1 to 32, as said below
- obs_owner: int32 [4, 8192, 1], P('member', 'lon'), parts along dimension 0, may hold values from 0 to 15; in each aligned block of 512 rows (0 to 511, 512 to 1023, ..., all dimensions but the last counted through in order) at most 64 rows name the same one
- obs_values: float32 [4, 16, 16, 64, 95], P('member', 'lon'), parts along dimension 0, may hold values from -6 to 6
- obs_precision: float32 [4, 16, 16, 64, 95], P('member', 'lon'), parts along dimension 0, may hold values from 0.5 to 2
Outputs:
- gradient: float32 [190, 256, 128], P('member', 'lon'), parts along dimension 0
The draws below stay inside these ranges and needn't reach their ends.
There are 2 independent parts, one for each index of `member`. The reference program is written for one: setup_inputs(seed, part) draws one part's arguments, and reference() takes and returns one part's arrays. A program takes and returns all parts, laid end to end along the dimension named above; an argument that names none is the same for every part. Nothing has to cross between parts.
Inputs may be any that keep to these rules, and one draw needn't show every extreme that they name: Slots k >= tile_counts of a tile are padding; some tile of every time holds 32 observations. `obs_owner`: within the 512 slots of one band at one time, no owner is named by more than 64 slots, and some band names one owner exactly 64 times.
All inputs are finite; a program needn't handle non-finite values.
Results may differ from the reference program's by a relative error of at most 0.015.
Values may be sent and summed in bfloat16 or wider, within the bound.
A program may use at most 128 MiB of HBM per device.

```python
import math
import jax
import jax.numpy as jnp
import numpy as np
from jax import lax

S = 95
C = 256
E = 1024
K = 32
P_SIZE = 4
TILE_CELLS = 128
LON_DEV = 16
LAT = 128
LON = 256
TILE_LAT = 8
TILES = 16
TILES_ALL = 256
CAP = 64
N_LON = 16


def draw_tile_counts(key, part):
    key_base, key_level, key_pick = jax.random.split(jax.random.fold_in(key, 17), 3)
    base_counts = jax.random.randint(key_base, (2, TILES_ALL), 1, K + 1)
    band_level = jax.random.randint(key_level, (2, TILES_ALL // TILES, 1), 1, 5)
    band_level = jnp.broadcast_to(band_level, (2, TILES_ALL // TILES, TILES)).reshape(2, TILES_ALL)
    counts = 1 + (base_counts - 1) * band_level // 4
    picked = jax.random.randint(key_pick, (2, 1), 0, TILES_ALL)
    spots = jnp.arange(TILES_ALL, dtype=jnp.int32)[None, :]
    return jnp.where(spots == picked, K, counts).astype(jnp.int32)


def place_ends(values, rng, low, high):
    shape = values.shape
    spot = [jax.random.randint(jax.random.fold_in(rng, axis), (), 0, shape[axis]) for axis in range(len(shape))]
    values = values.at[tuple(spot)].set(low)
    longest = shape.index(max(shape))
    spot[longest] = (spot[longest] + 1) % shape[longest]
    return values.at[tuple(spot)].set(high)


def steps_of(key, extent, cuts, low, top_value):
    level = 1.0
    for axis_at, blocks in cuts:
        heights = jax.random.uniform(jax.random.fold_in(jax.random.fold_in(key, 6), axis_at), (blocks,), jnp.float32, low / len(cuts), top_value / len(cuts))
        level = level * jnp.repeat(jnp.exp(heights), extent[axis_at] // blocks).reshape((-1,) + (1,) * (len(extent) - 1 - axis_at))
    return level


def shared_out(key, own, number, rows, amount, top, limit, lean):
    sequence = jax.random.permutation(key, amount)
    packed, common = portions_of(amount, rows * top, limit, lean, True), portions_of(amount, rows * top, limit, lean, False)
    places = jnp.arange(amount)

    def named(lengths, turn):
        used = int((lengths > 0).sum())
        fixed = max(1, used // 4)
        moved = fixed + (places - fixed + turn * (used - fixed)) % max(1, amount - fixed)
        return jnp.zeros((amount,), jnp.int32).at[sequence[jnp.where(places < fixed, places, moved)]].set(jnp.asarray(lengths, jnp.int32))

    lengths = jnp.where(number % 4 == 0, named(packed, number // 4), named(common, number - number // 4 - 1))
    mixed = jax.random.permutation(jax.random.fold_in(own, 3), amount)
    giver, sink = mixed[0:amount // 2 * 2:2], mixed[1:amount // 2 * 2:2]
    room = jnp.minimum(lengths[giver] - 1, limit - lengths[sink]) // 2
    room = jnp.where((giver == sequence[0]) | (sink == sequence[0]) | (lengths[sink] == 0), 0, jnp.maximum(room, 0))
    moved = jax.random.randint(jax.random.fold_in(own, 4), (amount // 2,), 0, 1 << 20) % (room + 1)
    lengths = lengths.at[giver].add(-moved).at[sink].add(moved)
    members = jnp.searchsorted(jnp.cumsum(lengths), jnp.arange(rows * top), side="right").astype(jnp.int32)
    grid = members.reshape(top, rows).T
    grid = grid[jax.random.permutation(jax.random.fold_in(own, 1), rows)]
    turn = jax.random.randint(jax.random.fold_in(own, 2), (rows, 1), 0, top)
    return jnp.take_along_axis(grid, (jnp.arange(top)[None, :] + turn) % top, axis=1)


def portions_of(number_of, total, reach, skew, full):
    loads = [(1 << 20) // math.isqrt(rank ** skew) + 1 for rank in range(1, number_of + 1)]
    largest = reach if full else min(reach, max(-(-total // number_of), total * loads[0] // sum(loads)))
    least = 1 if total - largest >= number_of - 1 else 0
    given, spare = [largest] + [least] * (number_of - 1), total - largest - least * (number_of - 1)
    while spare > 0:
        candidates = [i for i in range(1, number_of) if given[i] < largest] or [i for i in range(1, number_of) if given[i] < reach]
        pool, left = sum([loads[i] for i in candidates]), spare
        for i in candidates:
            addition = min(reach - given[i], max(1, left * loads[i] // pool), spare)
            given[i] = given[i] + addition
            spare = spare - addition
    return np.array(given)


def normal_values(own_key, shape, scale, bound, cuts=(), held_as=jnp.bfloat16):
    entries = scale * jax.random.normal(own_key, shape, jnp.float32)
    if cuts:
        entries = entries * steps_of(own_key, shape, cuts, -0.22, 0.18)
    return jnp.clip(entries, -bound, bound).astype(held_as)


def setup_inputs(seed: int = 0, part: int = 0) -> dict:
    seeds = jax.random.split(jax.random.key(seed), 14)
    part_splits = jax.random.split(jax.random.fold_in(seeds[13], part), 14)
    state_start = normal_values(part_splits[0], (S, LON, LAT), 1.0, 6.0, ((1, 16),), jnp.float32)
    lift_weight = normal_values(seeds[1], (S, C), S ** -0.5, 0.625)
    conv_kernel = normal_values(seeds[2], (49, C), 49 ** -0.5, 0.875, (), jnp.float32)
    norm_gain = jnp.clip(1.0 + 0.18 * jax.random.normal(seeds[3], (C,), jnp.float32), 0.1, 1.9)
    up_weight = normal_values(seeds[4], (C, E), C ** -0.5, 0.375)
    down_weight = normal_values(seeds[5], (E, C), E ** -0.5, 0.1875)
    out_weight = normal_values(seeds[6], (C, S), C ** -0.5, 0.375)
    obs_cells = place_ends(jax.random.randint(part_splits[7], (2, TILES_ALL, K, P_SIZE), 0, TILE_CELLS), jax.random.fold_in(part_splits[7], 1), 0, TILE_CELLS - 1).astype(jnp.int32)
    obs_weights = jnp.clip(jnp.exp(math.log(1.0) - 2.3025851 * jax.random.uniform(part_splits[8], (2, TILES_ALL, K, P_SIZE), jnp.float32) ** steps_of(part_splits[8], (2, TILES_ALL, K, P_SIZE), ((1, 16),), -0.2, 0.2)), 0.1, 1.0)
    tile_counts = draw_tile_counts(jax.random.fold_in(jax.random.fold_in(seeds[13], part), 71), part)
    obs_owner_keys = jax.random.split(jax.random.fold_in(part_splits[10], 1), 2 * (TILES_ALL * K) // (TILES * K))
    obs_owner_turns = jax.random.permutation(jax.random.fold_in(part_splits[10], 3), 2 * (TILES_ALL * K) // (TILES * K))
    obs_owner = jax.vmap(lambda own, number: shared_out(jax.random.fold_in(part_splits[10], 2), own, number, TILES * K, N_LON, 1, CAP, 2))(obs_owner_keys, obs_owner_turns).reshape((2, TILES_ALL * K, 1))
    obs_values = normal_values(part_splits[11], (2, N_LON, N_LON, CAP, S), 1.0, 6.0, ((1, 16),), jnp.float32)
    obs_precision = jnp.clip(jnp.exp(math.log(2.0) - 1.3862944 * jax.random.uniform(part_splits[12], (2, N_LON, N_LON, CAP, S), jnp.float32) ** steps_of(part_splits[12], (2, N_LON, N_LON, CAP, S), ((1, 16),), -0.2, 0.2)), 0.5, 2.0)
    return {"state_start": state_start, "lift_weight": lift_weight, "conv_kernel": conv_kernel, "norm_gain": norm_gain, "up_weight": up_weight, "down_weight": down_weight, "out_weight": out_weight, "obs_cells": obs_cells, "obs_weights": obs_weights, "tile_counts": tile_counts, "obs_owner": obs_owner, "obs_values": obs_values, "obs_precision": obs_precision}


gelu_coef = 0.044715
root_two_pi = 0.7978845608028654
eps_norm = 1e-06
highest = lax.Precision.HIGHEST

def half_dot(left, right):
    return jnp.dot(left.astype(jnp.float32), right.astype(jnp.float32), precision=highest)

def gelu_value(z):
    inner_arg = root_two_pi * (z + gelu_coef * z * z * z)
    return 0.5 * z * (1.0 + jnp.tanh(inner_arg))

def gelu_slope(z):
    inner_arg = root_two_pi * (z + gelu_coef * z * z * z)
    tanh_val = jnp.tanh(inner_arg)
    return 0.5 * (1.0 + tanh_val) + 0.5 * z * (1.0 - tanh_val * tanh_val) * root_two_pi * (1.0 + 3.0 * gelu_coef * z * z)

def wrap_pad(grid_field, margin):
    wrapped = jnp.concatenate([grid_field[-margin:], grid_field, grid_field[:margin]], axis=0)
    return jnp.pad(wrapped, ((0, 0), (margin, margin), (0, 0)))

def conv_taps(padded, kernel, lon_rows, lat_cols):
    summed = jnp.zeros((lon_rows, lat_cols, padded.shape[2]), jnp.float32)
    for i in range(7):
        for j in range(7):
            summed = summed + kernel[i * 7 + j] * padded[i:i + lon_rows, j:j + lat_cols].astype(jnp.float32)
    return summed

def conv_flip(padded, kernel, lon_rows, lat_cols):
    summed = jnp.zeros((lon_rows, lat_cols, padded.shape[2]), jnp.float32)
    for i in range(7):
        for j in range(7):
            summed = summed + kernel[i * 7 + j] * padded[6 - i:6 - i + lon_rows, 6 - j:6 - j + lat_cols]
    return summed

def model_step(state_field, weights):
    lift_weight, conv_kernel, norm_gain, up_weight, down_weight, out_weight = weights
    channels, lon_rows, lat_cols = state_field.shape
    hidden = lift_weight.shape[1]
    state_half = state_field.astype(jnp.bfloat16).reshape(channels, lon_rows * lat_cols)
    lifted = half_dot(state_half.T, lift_weight).astype(jnp.bfloat16)
    lifted = lifted.reshape(lon_rows, lat_cols, hidden)
    mixed_taps = conv_taps(wrap_pad(lifted, 3), conv_kernel, lon_rows, lat_cols)
    center = mixed_taps - lax.optimization_barrier(jnp.mean(mixed_taps, axis=2, keepdims=True))
    inverse = lax.rsqrt(lax.optimization_barrier(jnp.mean(center * center, axis=2, keepdims=True)) + eps_norm)
    normal = center * inverse
    normed = (normal * norm_gain).astype(jnp.bfloat16)

    def mlp_block(pieces):
        normed_part, lifted_part = pieces
        middle = half_dot(normed_part, up_weight)
        active = gelu_value(middle).astype(jnp.bfloat16)
        return (lifted_part.astype(jnp.float32) + half_dot(active, down_weight)).astype(jnp.bfloat16)
    block_out = lax.map(mlp_block, (normed.reshape(N_LON, -1, hidden), lifted.reshape(N_LON, -1, hidden)))
    change = half_dot(block_out.reshape(lon_rows * lat_cols, hidden), out_weight)
    return (state_field + change.T.reshape(channels, lon_rows, lat_cols), (normal, inverse, normed))

def step_adjoint(cotangent, saved, weights):
    lift_weight, conv_kernel, norm_gain, up_weight, down_weight, out_weight = weights
    normal, inverse, normed = saved
    channels, lon_rows, lat_cols = cotangent.shape
    hidden = lift_weight.shape[1]
    cot_half = cotangent.astype(jnp.bfloat16).reshape(channels, lon_rows * lat_cols)
    g_block = half_dot(cot_half.T, out_weight.T)

    def back_block(pieces):
        normed_part, block_part = pieces
        middle = half_dot(normed_part, up_weight)
        g_active = half_dot(block_part.astype(jnp.bfloat16), down_weight.T)
        g_middle = (g_active * gelu_slope(middle)).astype(jnp.bfloat16)
        return half_dot(g_middle, up_weight.T)
    g_normed = lax.map(back_block, (normed.reshape(N_LON, -1, hidden), g_block.reshape(N_LON, -1, hidden)))
    g_normed = g_normed.reshape(lon_rows, lat_cols, hidden)
    g_scaled = g_normed * norm_gain
    g_mixed = inverse * (g_scaled - lax.optimization_barrier(jnp.mean(g_scaled, axis=2, keepdims=True)) - normal * lax.optimization_barrier(jnp.mean(g_scaled * normal, axis=2, keepdims=True)))
    g_lifted = g_block.reshape(lon_rows, lat_cols, hidden) + conv_flip(wrap_pad(g_mixed, 3), conv_kernel, lon_rows, lat_cols)
    g_state = half_dot(g_lifted.reshape(lon_rows * lat_cols, hidden).astype(jnp.bfloat16), lift_weight.T)
    return cotangent + g_state.T.reshape(channels, lon_rows, lat_cols)

def tile_ops(cell_ids, point_weights):
    positions = jnp.arange(TILE_CELLS, dtype=jnp.int32)
    return lax.optimization_barrier(jnp.sum(point_weights[..., None] * (cell_ids[..., None] == positions).astype(jnp.float32), axis=2))

def to_tiles(state_field):
    channels, lon_rows, lat_cols = state_field.shape
    split = state_field.reshape(channels, N_LON, LON_DEV, TILES, TILE_LAT)
    return split.transpose(1, 3, 0, 2, 4).reshape(N_LON * TILES, channels, TILE_CELLS)

def from_tiles(tile_sums):
    channels = tile_sums.shape[1]
    split = tile_sums.reshape(N_LON, TILES, channels, LON_DEV, TILE_LAT)
    return split.transpose(2, 0, 3, 1, 4).reshape(channels, N_LON * LON_DEV, LAT)

def misfit_of(state_field, moment, operator, obs_owner, tile_counts, obs_values, obs_precision):
    channels = state_field.shape[0]
    model_equiv = jnp.einsum('gkc,gsc->gks', operator, to_tiles(state_field), precision=highest).reshape(-1, channels)
    per_band = TILES * K
    owner_ids = obs_owner[moment, :, 0]
    grouped = owner_ids.reshape(N_LON, per_band)
    onehot = (grouped[:, :, None] == jnp.arange(N_LON, dtype=jnp.int32)).astype(jnp.int32)
    before = jnp.cumsum(onehot, axis=1) - onehot
    place = lax.optimization_barrier(jnp.sum(before * onehot, axis=2)).reshape(-1).astype(jnp.int32)
    source = (jnp.arange(N_LON * per_band, dtype=jnp.int32) // per_band).astype(jnp.int32)
    target = obs_values[moment][owner_ids, source, place]
    weight_obs = obs_precision[moment][owner_ids, source, place]
    live_slots = (jnp.arange(K, dtype=jnp.int32)[None, :] < tile_counts[moment][:, None]).astype(jnp.float32).reshape(-1, 1)
    return live_slots * (weight_obs * (model_equiv - target))

def pull_back(operator, misfit):
    channels = misfit.shape[1]
    tile_sums = jnp.einsum('gkc,gks->gsc', operator, misfit.reshape(-1, K, channels), precision=highest)
    return from_tiles(tile_sums)

def reference(state_start, lift_weight, conv_kernel, norm_gain, up_weight, down_weight, out_weight, obs_cells, obs_weights, tile_counts, obs_owner, obs_values, obs_precision):
    weights = (lift_weight, conv_kernel, norm_gain, up_weight, down_weight, out_weight)
    state_one, saved_zero = model_step(state_start, weights)
    state_two, saved_one = model_step(state_one, weights)
    operator_one = tile_ops(obs_cells[0], obs_weights[0])
    operator_two = tile_ops(obs_cells[1], obs_weights[1])
    misfit_one = misfit_of(state_one, 0, operator_one, obs_owner, tile_counts, obs_values, obs_precision)
    misfit_two = misfit_of(state_two, 1, operator_two, obs_owner, tile_counts, obs_values, obs_precision)
    carried = step_adjoint(pull_back(operator_two, misfit_two), saved_one, weights) + pull_back(operator_one, misfit_one)
    return step_adjoint(carried, saved_zero, weights)
```

```python
import functools

import jax
import jax.numpy as jnp
from jax import lax
from jax.experimental import pallas as pl
from jax.experimental.pallas import tpu as pltpu
from jax.sharding import PartitionSpec as P

TILE_CELLS = 128


gelu_coef = 0.044715
root_two_pi = 0.7978845608028654
eps_norm = 1e-06
TAPS = 7
REACH = 3
VMEM_LIMIT = 56 * 1024 * 1024


def from_behind(value, axis, steps):
    count = lax.axis_size(axis)
    pairs = [(source, (source + steps) % count) for source in range(count)]
    return lax.ppermute(value, axis, pairs)


def edges(cells):
    west = from_behind(cells[-REACH:].astype(jnp.bfloat16), "lon", 1)
    east = from_behind(cells[:REACH].astype(jnp.bfloat16), "lon", -1)
    return west, east


def fill_padded(pad_ref, west_ref, mid_ref, east_ref):
    lon_rows, lat_cols, hidden = mid_ref.shape
    halves = hidden // 128
    zeros = jnp.zeros((8, 128), jnp.float32)

    def put(row, ref, at):
        for h in range(halves):
            pad_ref[h, row, 0:8, :] = zeros
            pad_ref[h, row, 8 + lat_cols : 16 + lat_cols, :] = zeros
            pad_ref[h, row, 8 : 8 + lat_cols, :] = ref[at, :, h * 128 : (h + 1) * 128].astype(
                jnp.float32
            )

    for row in range(REACH):
        put(row, west_ref, row)
        put(lon_rows + REACH + row, east_ref, row)

    def middle_row(row, carry):
        put(row + REACH, mid_ref, row)
        return carry

    lax.fori_loop(0, lon_rows, middle_row, 0)


def conv_block(pad_ref, kern_ref, mix_ref, lat_start):
    halves, lon_pad, _, _ = pad_ref.shape
    lon_rows = lon_pad - 2 * REACH

    def piece(step, carry):
        h, sub = step // 2, step % 2
        base = pl.multiple_of(lat_start + sub * 8, 8)
        sums = [None] * lon_rows
        for j in range(TAPS):
            weight = [kern_ref[h, i * TAPS + j] for i in range(TAPS)]
            for row in range(lon_pad):
                cells = pad_ref[h, row, pl.ds(base + j + 8 - REACH, 8), :]
                for i in range(TAPS):
                    o = row - i
                    if 0 <= o < lon_rows:
                        term = weight[i] * cells
                        sums[o] = term if sums[o] is None else sums[o] + term
        for o in range(lon_rows):
            mix_ref[h, o, pl.ds(pl.multiple_of(sub * 8, 8), 8), :] = sums[o]
        return carry

    lax.fori_loop(0, halves * 2, piece, 0)


def conv_norm_kernel(
    west_ref, mid_ref, east_ref, kern_ref, gain_ref, normal_ref, normed_ref, inverse_ref, pad_ref, mix_ref
):
    lon_rows, lat_cols, hidden = mid_ref.shape
    fill_padded(pad_ref, west_ref, mid_ref, east_ref)

    def block(at, carry):
        lat = pl.multiple_of(at * 16, 16)
        conv_block(pad_ref, kern_ref, mix_ref, lat)
        gain = gain_ref[...]
        for o in range(lon_rows):
            mixed = jnp.concatenate([mix_ref[h, o] for h in range(hidden // 128)], axis=1)
            center = mixed - jnp.mean(mixed, axis=1, keepdims=True)
            inverse = lax.rsqrt(jnp.mean(center * center, axis=1, keepdims=True) + eps_norm)
            normal = center * inverse
            normal_ref[o, pl.ds(lat, 16), :] = normal
            normed_ref[o, pl.ds(lat, 16), :] = (normal * gain).astype(jnp.bfloat16)
            inverse_ref[o, pl.ds(lat, 16), :] = jnp.broadcast_to(inverse, (16, 128))
        return carry

    lax.fori_loop(0, lat_cols // 16, block, 0)


def conv_add_kernel(west_ref, mid_ref, east_ref, kern_ref, add_ref, out_ref, pad_ref, mix_ref):
    lon_rows, lat_cols, hidden = mid_ref.shape
    fill_padded(pad_ref, west_ref, mid_ref, east_ref)

    def block(at, carry):
        lat = pl.multiple_of(at * 16, 16)
        conv_block(pad_ref, kern_ref, mix_ref, lat)
        for o in range(lon_rows):
            summed = jnp.concatenate([mix_ref[h, o] for h in range(hidden // 128)], axis=1)
            out_ref[o, pl.ds(lat, 16), :] = (add_ref[o, pl.ds(lat, 16), :] + summed).astype(
                jnp.bfloat16
            )
        return carry

    lax.fori_loop(0, lat_cols // 16, block, 0)


def conv_scratch(shape):
    lon_rows, lat_cols, hidden = shape
    halves = hidden // 128
    return [
        pltpu.VMEM((halves, lon_rows + 2 * REACH, lat_cols + 16, 128), jnp.float32),
        pltpu.VMEM((halves, lon_rows, 16, 128), jnp.float32),
    ]


def conv_cost(shape):
    cells = shape[0] * shape[1] * shape[2]
    return pl.CostEstimate(flops=cells * 98, bytes_accessed=cells * 12, transcendentals=0)


def in_vmem(count):
    return [pl.BlockSpec(memory_space=pltpu.VMEM)] * count


def conv_norm(cells, kern, gain):
    west, east = edges(cells)
    shape = cells.shape
    return pl.pallas_call(
        conv_norm_kernel,
        out_shape=(
            jax.ShapeDtypeStruct(shape, jnp.float32),
            jax.ShapeDtypeStruct(shape, jnp.bfloat16),
            jax.ShapeDtypeStruct(shape[:2] + (128,), jnp.float32),
        ),
        in_specs=in_vmem(5),
        out_specs=tuple(in_vmem(3)),
        scratch_shapes=conv_scratch(shape),
        cost_estimate=conv_cost(shape),
        compiler_params=pltpu.CompilerParams(vmem_limit_bytes=VMEM_LIMIT),
    )(west, cells, east, kern, gain)


def conv_add(cells, kern, add):
    west, east = edges(cells)
    shape = cells.shape
    return pl.pallas_call(
        conv_add_kernel,
        out_shape=jax.ShapeDtypeStruct(shape, jnp.bfloat16),
        in_specs=in_vmem(5),
        out_specs=pl.BlockSpec(memory_space=pltpu.VMEM),
        scratch_shapes=conv_scratch(shape),
        cost_estimate=conv_cost(shape),
        compiler_params=pltpu.CompilerParams(vmem_limit_bytes=VMEM_LIMIT),
    )(west, cells, east, kern, add)


def mlp_kernel(piece, normed_ref, lifted_ref, up_ref, down_ref, block_ref, slope_ref):
    normed = normed_ref[...]
    total = lifted_ref[...].astype(jnp.float32)
    for start in range(0, up_ref.shape[1], piece):
        z = jnp.dot(normed, up_ref[:, start : start + piece], preferred_element_type=jnp.float32)
        square = z * z
        tanh_val = jnp.tanh(z * (root_two_pi + root_two_pi * gelu_coef * square))
        half = 0.5 + 0.5 * tanh_val
        active = (z * half).astype(jnp.bfloat16)
        bend = z * (root_two_pi + 3.0 * root_two_pi * gelu_coef * square)
        slope = half + half * (1.0 - tanh_val) * bend
        slope_ref[:, start : start + piece] = slope.astype(jnp.bfloat16)
        total = total + jnp.dot(
            active, down_ref[start : start + piece, :], preferred_element_type=jnp.float32
        )
    block_ref[...] = total.astype(jnp.bfloat16)


def mlp(normed, lifted, up_weight, down_weight, rows=512, piece=256):
    amount, hidden = normed.shape
    wide = up_weight.shape[1]
    by_rows = lambda width: pl.BlockSpec((rows, width), lambda r: (r, 0))
    whole = lambda shape: pl.BlockSpec(shape, lambda r: (0, 0))
    return pl.pallas_call(
        functools.partial(mlp_kernel, piece),
        grid=(amount // rows,),
        out_shape=(
            jax.ShapeDtypeStruct((amount, hidden), jnp.bfloat16),
            jax.ShapeDtypeStruct((amount, wide), jnp.bfloat16),
        ),
        in_specs=[by_rows(hidden), by_rows(hidden), whole((hidden, wide)), whole((wide, hidden))],
        out_specs=(by_rows(hidden), by_rows(wide)),
        cost_estimate=pl.CostEstimate(
            flops=4 * amount * hidden * wide,
            bytes_accessed=amount * (wide + 3 * hidden) * 2,
            transcendentals=amount * wide,
        ),
        compiler_params=pltpu.CompilerParams(vmem_limit_bytes=VMEM_LIMIT),
    )(normed, lifted, up_weight, down_weight)


def mlp_back_kernel(
    piece, block_ref, slope_ref, normal_ref, inverse_ref, gain_ref, up_ref, down_ref, out_ref
):
    g_block = block_ref[...].astype(jnp.bfloat16)
    across = (((1,), (1,)), ((), ()))
    total = None
    for start in range(0, up_ref.shape[1], piece):
        g_active = lax.dot_general(
            g_block,
            down_ref[start : start + piece, :],
            across,
            preferred_element_type=jnp.float32,
        )
        g_middle = g_active * slope_ref[:, start : start + piece].astype(jnp.float32)
        term = lax.dot_general(
            g_middle.astype(jnp.bfloat16),
            up_ref[:, start : start + piece],
            across,
            preferred_element_type=jnp.float32,
        )
        total = term if total is None else total + term
    g_scaled = total * gain_ref[...]
    normal = normal_ref[...]
    out_ref[...] = inverse_ref[:, 0:1] * (
        g_scaled
        - jnp.mean(g_scaled, axis=1, keepdims=True)
        - normal * jnp.mean(g_scaled * normal, axis=1, keepdims=True)
    )


def mlp_back(g_block, slope, normal, inverse, gain, up_weight, down_weight, rows=512, piece=256):
    amount, hidden = g_block.shape
    wide = up_weight.shape[1]
    by_rows = lambda width: pl.BlockSpec((rows, width), lambda r: (r, 0))
    whole = lambda shape: pl.BlockSpec(shape, lambda r: (0, 0))
    return pl.pallas_call(
        functools.partial(mlp_back_kernel, piece),
        grid=(amount // rows,),
        out_shape=jax.ShapeDtypeStruct((amount, hidden), jnp.float32),
        in_specs=[
            by_rows(hidden),
            by_rows(wide),
            by_rows(hidden),
            by_rows(128),
            whole((1, hidden)),
            whole((hidden, wide)),
            whole((wide, hidden)),
        ],
        out_specs=by_rows(hidden),
        cost_estimate=pl.CostEstimate(
            flops=4 * amount * hidden * wide,
            bytes_accessed=amount * (2 * wide + 12 * hidden),
            transcendentals=0,
        ),
        compiler_params=pltpu.CompilerParams(vmem_limit_bytes=VMEM_LIMIT),
    )(g_block, slope, normal, inverse, gain, up_weight, down_weight)


def forward_step(state_field, weights):
    lift_weight, kern, _, gain, up_weight, down_weight, out_weight = weights
    channels, lon_rows, lat_cols = state_field.shape
    hidden = lift_weight.shape[1]
    lifted = lax.dot_general(
        state_field.astype(jnp.bfloat16),
        lift_weight,
        (((0,), (0,)), ((), ())),
        preferred_element_type=jnp.float32,
    ).astype(jnp.bfloat16)
    normal, normed, inverse = conv_norm(lifted, kern, gain)
    block_out, slope = mlp(
        normed.reshape(-1, hidden), lifted.reshape(-1, hidden), up_weight, down_weight
    )
    change = lax.dot_general(
        out_weight, block_out, (((0,), (1,)), ((), ())), preferred_element_type=jnp.float32
    )
    saved = (normal.reshape(-1, hidden), inverse.reshape(-1, 128), slope)
    return state_field + change.reshape(channels, lon_rows, lat_cols), saved


def backward_step(cotangent, saved, weights):
    lift_weight, _, flipped, gain, up_weight, down_weight, out_weight = weights
    normal, inverse, slope = saved
    channels, lon_rows, lat_cols = cotangent.shape
    hidden = lift_weight.shape[1]
    g_block = lax.dot_general(
        cotangent.astype(jnp.bfloat16),
        out_weight,
        (((0,), (1,)), ((), ())),
        preferred_element_type=jnp.float32,
    )
    g_mixed = mlp_back(
        g_block.reshape(-1, hidden), slope, normal, inverse, gain, up_weight, down_weight
    ).reshape(lon_rows, lat_cols, hidden)
    g_lifted = conv_add(g_mixed, flipped, g_block)
    g_state = lax.dot_general(
        lift_weight, g_lifted, (((1,), (2,)), ((), ())), preferred_element_type=jnp.float32
    )
    return cotangent + g_state


def tile_ops(cell_ids, point_weights):
    positions = jnp.arange(TILE_CELLS, dtype=jnp.int32)
    return jnp.sum(
        point_weights[..., None] * (cell_ids[..., None] == positions).astype(jnp.float32), axis=2
    )


def to_tiles(state_field):
    channels, lon_rows, lat_cols = state_field.shape
    tile_rows = TILE_CELLS // lon_rows
    split = state_field.reshape(channels, lon_rows, lat_cols // tile_rows, tile_rows)
    return split.transpose(2, 0, 1, 3).reshape(lat_cols // tile_rows, channels, TILE_CELLS)


def from_tiles(tile_sums, lon_rows):
    tile_total, channels, _ = tile_sums.shape
    tile_rows = TILE_CELLS // lon_rows
    split = tile_sums.reshape(tile_total, channels, lon_rows, tile_rows)
    return split.transpose(1, 2, 0, 3).reshape(channels, lon_rows, tile_total * tile_rows)


def slot_selector(owner_ids, band_count, place_count):
    hit = owner_ids[:, None] == jnp.arange(band_count, dtype=jnp.int32)[None, :]
    slots = jnp.arange(owner_ids.shape[0], dtype=jnp.int32)
    earlier = (slots[None, :] < slots[:, None]).astype(jnp.bfloat16)
    before = jnp.dot(earlier, hit.astype(jnp.bfloat16), preferred_element_type=jnp.float32)
    place = jnp.sum(jnp.where(hit, before, 0.0), axis=1).astype(jnp.int32)
    slot_code = owner_ids * place_count + place
    return (
        slot_code[:, None] == jnp.arange(band_count * place_count, dtype=jnp.int32)[None, :]
    ).astype(jnp.bfloat16)


def owners_data(obs_values, obs_precision):
    channels = obs_values.shape[-1]
    widen = ((0, 0), (0, 0), (0, 0), (0, 128 - channels))
    both = jnp.concatenate(
        [jnp.pad(part[:, 0].astype(jnp.bfloat16), widen) for part in (obs_values, obs_precision)],
        axis=3,
    ).transpose(1, 0, 2, 3)
    return lax.all_to_all(both, "lon", split_axis=0, concat_axis=0, tiled=True)


def shards(
    state_start,
    lift_weight,
    conv_kernel,
    norm_gain,
    up_weight,
    down_weight,
    out_weight,
    obs_cells,
    obs_weights,
    tile_counts,
    obs_owner,
    obs_values,
    obs_precision,
):
    hidden = norm_gain.shape[0]
    by_half = lambda taps: jnp.broadcast_to(
        taps.reshape(-1, 1, hidden // 128, 128).transpose(2, 0, 1, 3),
        (hidden // 128, taps.shape[0], 8, 128),
    )
    weights = (
        lift_weight,
        by_half(conv_kernel),
        by_half(conv_kernel[::-1]),
        norm_gain.reshape(1, hidden),
        up_weight,
        down_weight,
        out_weight,
    )
    channels, lon_rows = (state_start.shape[0], state_start.shape[1])
    band_count, place_count = (obs_values.shape[2], obs_values.shape[3])
    tile_total, slot_total = (obs_cells.shape[1], obs_cells.shape[2])
    arrived = owners_data(obs_values, obs_precision)
    operators = [
        tile_ops(obs_cells[moment], obs_weights[moment]).astype(jnp.bfloat16) for moment in range(2)
    ]
    state_one, saved_zero = forward_step(state_start, weights)
    state_two, saved_one = forward_step(state_one, weights)

    def pulled(moment, state_field):
        selector = slot_selector(obs_owner[moment, :, 0], band_count, place_count)
        chosen = jnp.dot(
            selector,
            arrived[:, moment].reshape(band_count * place_count, -1),
            preferred_element_type=jnp.float32,
        )
        live_slots = (
            (jnp.arange(slot_total, dtype=jnp.int32)[None, :] < tile_counts[moment][:, None])
            .astype(jnp.float32)
            .reshape(-1, 1)
        )
        model_equiv = jnp.einsum(
            "gkc,gsc->gks",
            operators[moment],
            to_tiles(state_field.astype(jnp.bfloat16)),
            preferred_element_type=jnp.float32,
        ).reshape(-1, channels)
        misfit = live_slots * (
            chosen[:, 128 : 128 + channels] * (model_equiv - chosen[:, :channels])
        )
        tile_sums = jnp.einsum(
            "gkc,gks->gsc",
            operators[moment],
            misfit.reshape(tile_total, slot_total, channels).astype(jnp.bfloat16),
            preferred_element_type=jnp.float32,
        )
        return from_tiles(tile_sums, lon_rows)

    carried = backward_step(pulled(1, state_two), saved_one, weights) + pulled(0, state_one)
    return backward_step(carried, saved_zero, weights)


def solution(mesh):
    placed = (
        P("member", "lon", None),
        P(),
        P(),
        P(),
        P(),
        P(),
        P(),
        P("member", "lon", None, None),
        P("member", "lon", None, None),
        P("member", "lon"),
        P("member", "lon", None),
        P("member", "lon", None, None, None),
        P("member", "lon", None, None, None),
    )
    return jax.shard_map(
        shards, mesh=mesh, in_specs=placed, out_specs=P("member", "lon", None), check_vma=False
    )
```

```python
import functools

import jax
import jax.numpy as jnp
from jax import lax
from jax.experimental import pallas as pl
from jax.experimental.pallas import tpu as pltpu
from jax.sharding import PartitionSpec as P

TILE_CELLS = 128


gelu_coef = 0.044715
root_two_pi = 0.7978845608028654
eps_norm = 1e-06
TAPS = 7
REACH = 3
VMEM_LIMIT = 56 * 1024 * 1024


def exchange(mid_ref, west_ref, east_ref, send_sem, recv_sem):
    lon_rows = mid_ref.shape[0]
    count = lax.axis_size("lon")
    here = lax.axis_index("lon")
    ahead, behind = lax.rem(here + 1, count), lax.rem(here + count - 1, count)
    barrier = pltpu.get_barrier_semaphore()
    for neighbour in (behind, ahead):
        pl.semaphore_signal(
            barrier,
            inc=1,
            device_id={"lon": neighbour},
            device_id_type=pl.DeviceIdType.MESH,
        )
    pl.semaphore_wait(barrier, 2)
    copies = []
    for at, (source, target, neighbour) in enumerate(
        (
            (mid_ref.at[pl.ds(lon_rows - REACH, REACH)], west_ref, ahead),
            (mid_ref.at[pl.ds(0, REACH)], east_ref, behind),
        )
    ):
        copy = pltpu.make_async_remote_copy(
            src_ref=source,
            dst_ref=target,
            send_sem=send_sem.at[at],
            recv_sem=recv_sem.at[at],
            device_id={"lon": neighbour},
            device_id_type=pl.DeviceIdType.MESH,
        )
        copy.start()
        copies.append(copy)
    return copies


def put_row(pad_ref, row, ref, at):
    lat_cols, hidden = ref.shape[1:]
    zeros = jnp.zeros((8, 128), jnp.float32)
    for h in range(hidden // 128):
        pad_ref[h, row, 0:8, :] = zeros
        pad_ref[h, row, 8 + lat_cols : 16 + lat_cols, :] = zeros
        pad_ref[h, row, 8 : 8 + lat_cols, :] = ref[at, :, h * 128 : (h + 1) * 128].astype(
            jnp.float32
        )


def conv_block(pad_ref, kern_ref, mix_ref, lat_start, wanted, flip):
    halves, lon_pad, _, _ = pad_ref.shape
    last = TAPS * TAPS - 1

    def piece(step, carry):
        h, sub = step // 2, step % 2
        base = pl.multiple_of(lat_start + sub * 8, 8)
        sums = {}
        for j in range(TAPS):
            taps = [i * TAPS + j for i in range(TAPS)]
            weight = [kern_ref[h, last - tap if flip else tap] for tap in taps]
            for row in range(lon_pad):
                users = [(i, row - i) for i in range(TAPS) if row - i in wanted]
                if not users:
                    continue
                cells = pad_ref[h, row, pl.ds(base + j + 8 - REACH, 8), :]
                for i, o in users:
                    term = weight[i] * cells
                    sums[o] = sums[o] + term if o in sums else term
        for o in wanted:
            mix_ref[h, o, pl.ds(pl.multiple_of(sub * 8, 8), 8), :] = sums[o]
        return carry

    lax.fori_loop(0, halves * 2, piece, 0)


def conv_all(mid_ref, kern_ref, pad_ref, mix_ref, west_ref, east_ref, sems, flip, finish):
    lon_rows, lat_cols, _ = mid_ref.shape
    copies = exchange(mid_ref, west_ref, east_ref, *sems)

    def middle_row(row, carry):
        put_row(pad_ref, row + REACH, mid_ref, row)
        return carry

    lax.fori_loop(0, lon_rows, middle_row, 0)
    inner = tuple(range(REACH, lon_rows - REACH))
    outer = tuple(o for o in range(lon_rows) if o not in inner)
    blocks = lat_cols // 16

    def run(first, end, wanted):
        def block(at, carry):
            lat = pl.multiple_of(at * 16, 16)
            conv_block(pad_ref, kern_ref, mix_ref, lat, wanted, flip)
            for o in wanted:
                halves = [mix_ref[h, o] for h in range(mix_ref.shape[0])]
                finish(o, lat, jnp.concatenate(halves, axis=1))
            return carry

        lax.fori_loop(first, end, block, 0)

    run(0, blocks // 2, inner)
    for copy in copies:
        copy.wait()
    for row in range(REACH):
        put_row(pad_ref, row, west_ref, row)
        put_row(pad_ref, lon_rows + REACH + row, east_ref, row)
    run(0, blocks // 2, outer)
    run(blocks // 2, blocks, tuple(range(lon_rows)))


def conv_norm_kernel(
    mid_ref,
    kern_ref,
    gain_ref,
    normal_ref,
    normed_ref,
    inverse_ref,
    pad_ref,
    mix_ref,
    west_ref,
    east_ref,
    *sems,
):
    def finish(o, lat, mixed):
        center = mixed - jnp.mean(mixed, axis=1, keepdims=True)
        inverse = lax.rsqrt(jnp.mean(center * center, axis=1, keepdims=True) + eps_norm)
        normal = center * inverse
        normal_ref[o, pl.ds(lat, 16), :] = normal.astype(jnp.bfloat16)
        normed_ref[o, pl.ds(lat, 16), :] = (normal * gain_ref[...]).astype(jnp.bfloat16)
        inverse_ref[o, pl.ds(lat, 16), :] = jnp.broadcast_to(inverse, (16, 128))

    conv_all(mid_ref, kern_ref, pad_ref, mix_ref, west_ref, east_ref, sems, False, finish)


def conv_add_kernel(
    mid_ref, kern_ref, add_ref, out_ref, pad_ref, mix_ref, west_ref, east_ref, *sems
):
    def finish(o, lat, summed):
        total = add_ref[o, pl.ds(lat, 16), :].astype(jnp.float32) + summed
        out_ref[o, pl.ds(lat, 16), :] = total.astype(jnp.bfloat16)

    conv_all(mid_ref, kern_ref, pad_ref, mix_ref, west_ref, east_ref, sems, True, finish)


def conv_scratch(shape):
    lon_rows, lat_cols, hidden = shape
    halves = hidden // 128
    return [
        pltpu.VMEM((halves, lon_rows + 2 * REACH, lat_cols + 16, 128), jnp.float32),
        pltpu.VMEM((halves, lon_rows, 16, 128), jnp.float32),
        pltpu.VMEM((REACH, lat_cols, hidden), jnp.bfloat16),
        pltpu.VMEM((REACH, lat_cols, hidden), jnp.bfloat16),
        pltpu.SemaphoreType.DMA((2,)),
        pltpu.SemaphoreType.DMA((2,)),
    ]


def conv_cost(shape):
    cells = shape[0] * shape[1] * shape[2]
    return pl.CostEstimate(flops=cells * 98, bytes_accessed=cells * 12, transcendentals=0)


def in_vmem(count):
    return [pl.BlockSpec(memory_space=pltpu.VMEM)] * count


def conv_norm(cells, kern, gain):
    shape = cells.shape
    return pl.pallas_call(
        conv_norm_kernel,
        out_shape=(
            jax.ShapeDtypeStruct(shape, jnp.bfloat16),
            jax.ShapeDtypeStruct(shape, jnp.bfloat16),
            jax.ShapeDtypeStruct(shape[:2] + (128,), jnp.float32),
        ),
        in_specs=in_vmem(3),
        out_specs=tuple(in_vmem(3)),
        scratch_shapes=conv_scratch(shape),
        cost_estimate=conv_cost(shape),
        compiler_params=pltpu.CompilerParams(
            vmem_limit_bytes=VMEM_LIMIT, collective_id=0, has_side_effects=True
        ),
    )(cells, kern, gain)


def conv_add(cells, kern, add):
    shape = cells.shape
    return pl.pallas_call(
        conv_add_kernel,
        out_shape=jax.ShapeDtypeStruct(shape, jnp.bfloat16),
        in_specs=in_vmem(3),
        out_specs=pl.BlockSpec(memory_space=pltpu.VMEM),
        scratch_shapes=conv_scratch(shape),
        cost_estimate=conv_cost(shape),
        compiler_params=pltpu.CompilerParams(
            vmem_limit_bytes=VMEM_LIMIT, collective_id=1, has_side_effects=True
        ),
    )(cells, kern, add)


def mlp_kernel(piece, normed_ref, lifted_ref, up_ref, down_ref, block_ref, slope_ref):
    normed = normed_ref[...]
    total = lifted_ref[...].astype(jnp.float32)
    for start in range(0, up_ref.shape[1], piece):
        z = jnp.dot(normed, up_ref[:, start : start + piece], preferred_element_type=jnp.float32)
        square = z * z
        tanh_val = jnp.tanh(z * (root_two_pi + root_two_pi * gelu_coef * square))
        half = 0.5 + 0.5 * tanh_val
        active = (z * half).astype(jnp.bfloat16)
        bend = z * (root_two_pi + 3.0 * root_two_pi * gelu_coef * square)
        slope = half + half * (1.0 - tanh_val) * bend
        slope_ref[:, start : start + piece] = slope.astype(jnp.bfloat16)
        total = total + jnp.dot(
            active, down_ref[start : start + piece, :], preferred_element_type=jnp.float32
        )
    block_ref[...] = total.astype(jnp.bfloat16)


def mlp(normed, lifted, up_weight, down_weight, rows=512, piece=256):
    amount, hidden = normed.shape
    wide = up_weight.shape[1]
    by_rows = lambda width: pl.BlockSpec((rows, width), lambda r: (r, 0))
    whole = lambda shape: pl.BlockSpec(shape, lambda r: (0, 0))
    return pl.pallas_call(
        functools.partial(mlp_kernel, piece),
        grid=(amount // rows,),
        out_shape=(
            jax.ShapeDtypeStruct((amount, hidden), jnp.bfloat16),
            jax.ShapeDtypeStruct((amount, wide), jnp.bfloat16),
        ),
        in_specs=[by_rows(hidden), by_rows(hidden), whole((hidden, wide)), whole((wide, hidden))],
        out_specs=(by_rows(hidden), by_rows(wide)),
        cost_estimate=pl.CostEstimate(
            flops=4 * amount * hidden * wide,
            bytes_accessed=amount * (wide + 3 * hidden) * 2,
            transcendentals=amount * wide,
        ),
        compiler_params=pltpu.CompilerParams(vmem_limit_bytes=VMEM_LIMIT),
    )(normed, lifted, up_weight, down_weight)


def mlp_back_kernel(
    piece, block_ref, slope_ref, normal_ref, inverse_ref, gain_ref, up_ref, down_ref, out_ref
):
    g_block = block_ref[...]
    across = (((1,), (1,)), ((), ()))
    total = None
    for start in range(0, up_ref.shape[1], piece):
        g_active = lax.dot_general(
            g_block,
            down_ref[start : start + piece, :],
            across,
            preferred_element_type=jnp.float32,
        )
        g_middle = g_active * slope_ref[:, start : start + piece].astype(jnp.float32)
        term = lax.dot_general(
            g_middle.astype(jnp.bfloat16),
            up_ref[:, start : start + piece],
            across,
            preferred_element_type=jnp.float32,
        )
        total = term if total is None else total + term
    g_scaled = total * gain_ref[...]
    normal = normal_ref[...].astype(jnp.float32)
    g_mixed = inverse_ref[:, 0:1] * (
        g_scaled
        - jnp.mean(g_scaled, axis=1, keepdims=True)
        - normal * jnp.mean(g_scaled * normal, axis=1, keepdims=True)
    )
    out_ref[...] = g_mixed.astype(jnp.bfloat16)


def mlp_back(g_block, slope, normal, inverse, gain, up_weight, down_weight, rows=512, piece=256):
    amount, hidden = g_block.shape
    wide = up_weight.shape[1]
    by_rows = lambda width: pl.BlockSpec((rows, width), lambda r: (r, 0))
    whole = lambda shape: pl.BlockSpec(shape, lambda r: (0, 0))
    return pl.pallas_call(
        functools.partial(mlp_back_kernel, piece),
        grid=(amount // rows,),
        out_shape=jax.ShapeDtypeStruct((amount, hidden), jnp.bfloat16),
        in_specs=[
            by_rows(hidden),
            by_rows(wide),
            by_rows(hidden),
            by_rows(128),
            whole((1, hidden)),
            whole((hidden, wide)),
            whole((wide, hidden)),
        ],
        out_specs=by_rows(hidden),
        cost_estimate=pl.CostEstimate(
            flops=4 * amount * hidden * wide,
            bytes_accessed=amount * (2 * wide + 8 * hidden),
            transcendentals=0,
        ),
        compiler_params=pltpu.CompilerParams(vmem_limit_bytes=VMEM_LIMIT),
    )(g_block, slope, normal, inverse, gain, up_weight, down_weight)


def forward_step(state_field, weights):
    lift_weight, kern, gain, up_weight, down_weight, out_weight = weights
    channels, lon_rows, lat_cols = state_field.shape
    hidden = lift_weight.shape[1]
    lifted = lax.dot_general(
        state_field.astype(jnp.bfloat16),
        lift_weight,
        (((0,), (0,)), ((), ())),
        preferred_element_type=jnp.float32,
    ).astype(jnp.bfloat16)
    normal, normed, inverse = conv_norm(lifted, kern, gain)
    block_out, slope = mlp(
        normed.reshape(-1, hidden), lifted.reshape(-1, hidden), up_weight, down_weight
    )
    change = lax.dot_general(
        out_weight, block_out, (((0,), (1,)), ((), ())), preferred_element_type=jnp.float32
    )
    saved = (normal.reshape(-1, hidden), inverse.reshape(-1, 128), slope)
    return state_field + change.reshape(channels, lon_rows, lat_cols), saved


def backward_step(cotangent, saved, weights):
    lift_weight, kern, gain, up_weight, down_weight, out_weight = weights
    normal, inverse, slope = saved
    channels, lon_rows, lat_cols = cotangent.shape
    hidden = lift_weight.shape[1]
    g_block = lax.dot_general(
        cotangent.astype(jnp.bfloat16),
        out_weight,
        (((0,), (1,)), ((), ())),
        preferred_element_type=jnp.float32,
    ).astype(jnp.bfloat16)
    g_mixed = mlp_back(
        g_block.reshape(-1, hidden), slope, normal, inverse, gain, up_weight, down_weight
    ).reshape(lon_rows, lat_cols, hidden)
    g_lifted = conv_add(g_mixed, kern, g_block)
    g_state = lax.dot_general(
        lift_weight, g_lifted, (((1,), (2,)), ((), ())), preferred_element_type=jnp.float32
    )
    return cotangent + g_state


def tile_ops(cell_ids, point_weights):
    positions = jnp.arange(TILE_CELLS, dtype=jnp.int32)
    return jnp.sum(
        point_weights[..., None] * (cell_ids[..., None] == positions).astype(jnp.float32), axis=2
    )


def to_tiles(state_field):
    channels, lon_rows, lat_cols = state_field.shape
    tile_rows = TILE_CELLS // lon_rows
    split = state_field.reshape(channels, lon_rows, lat_cols // tile_rows, tile_rows)
    return split.transpose(2, 0, 1, 3).reshape(lat_cols // tile_rows, channels, TILE_CELLS)


def from_tiles(tile_sums, lon_rows):
    tile_total, channels, _ = tile_sums.shape
    tile_rows = TILE_CELLS // lon_rows
    split = tile_sums.reshape(tile_total, channels, lon_rows, tile_rows)
    return split.transpose(1, 2, 0, 3).reshape(channels, lon_rows, tile_total * tile_rows)


def slot_selector(owner_ids, band_count, place_count):
    hit = owner_ids[:, None] == jnp.arange(band_count, dtype=jnp.int32)[None, :]
    slots = jnp.arange(owner_ids.shape[0], dtype=jnp.int32)
    earlier = (slots[None, :] < slots[:, None]).astype(jnp.bfloat16)
    before = jnp.dot(earlier, hit.astype(jnp.bfloat16), preferred_element_type=jnp.float32)
    place = jnp.sum(jnp.where(hit, before, 0.0), axis=1).astype(jnp.int32)
    slot_code = owner_ids * place_count + place
    return (
        slot_code[:, None] == jnp.arange(band_count * place_count, dtype=jnp.int32)[None, :]
    ).astype(jnp.bfloat16)


def owners_data(obs_values, obs_precision):
    channels = obs_values.shape[-1]
    widen = ((0, 0), (0, 0), (0, 0), (0, 128 - channels))
    both = jnp.concatenate(
        [jnp.pad(part[:, 0].astype(jnp.bfloat16), widen) for part in (obs_values, obs_precision)],
        axis=3,
    ).transpose(1, 0, 2, 3)
    return lax.all_to_all(both, "lon", split_axis=0, concat_axis=0, tiled=True)


def shards(
    state_start,
    lift_weight,
    conv_kernel,
    norm_gain,
    up_weight,
    down_weight,
    out_weight,
    obs_cells,
    obs_weights,
    tile_counts,
    obs_owner,
    obs_values,
    obs_precision,
):
    hidden = norm_gain.shape[0]
    by_half = lambda taps: jnp.broadcast_to(
        taps.reshape(-1, 1, hidden // 128, 128).transpose(2, 0, 1, 3),
        (hidden // 128, taps.shape[0], 8, 128),
    )
    weights = (
        lift_weight,
        by_half(conv_kernel),
        norm_gain.reshape(1, hidden),
        up_weight,
        down_weight,
        out_weight,
    )
    channels, lon_rows = (state_start.shape[0], state_start.shape[1])
    band_count, place_count = (obs_values.shape[2], obs_values.shape[3])
    tile_total, slot_total = (obs_cells.shape[1], obs_cells.shape[2])
    arrived = owners_data(obs_values, obs_precision)
    operators = [
        tile_ops(obs_cells[moment], obs_weights[moment]).astype(jnp.bfloat16) for moment in range(2)
    ]
    state_one, saved_zero = forward_step(state_start, weights)
    state_two, saved_one = forward_step(state_one, weights)

    def pulled(moment, state_field):
        selector = slot_selector(obs_owner[moment, :, 0], band_count, place_count)
        chosen = jnp.dot(
            selector,
            arrived[:, moment].reshape(band_count * place_count, -1),
            preferred_element_type=jnp.float32,
        )
        live_slots = (
            (jnp.arange(slot_total, dtype=jnp.int32)[None, :] < tile_counts[moment][:, None])
            .astype(jnp.float32)
            .reshape(-1, 1)
        )
        model_equiv = jnp.einsum(
            "gkc,gsc->gks",
            operators[moment],
            to_tiles(state_field.astype(jnp.bfloat16)),
            preferred_element_type=jnp.float32,
        ).reshape(-1, channels)
        misfit = live_slots * (
            chosen[:, 128 : 128 + channels] * (model_equiv - chosen[:, :channels])
        )
        tile_sums = jnp.einsum(
            "gkc,gks->gsc",
            operators[moment],
            misfit.reshape(tile_total, slot_total, channels).astype(jnp.bfloat16),
            preferred_element_type=jnp.float32,
        )
        return from_tiles(tile_sums, lon_rows)

    carried = backward_step(pulled(1, state_two), saved_one, weights) + pulled(0, state_one)
    return backward_step(carried, saved_zero, weights)


def solution(mesh):
    placed = (
        P("member", "lon", None),
        P(),
        P(),
        P(),
        P(),
        P(),
        P(),
        P("member", "lon", None, None),
        P("member", "lon", None, None),
        P("member", "lon"),
        P("member", "lon", None),
        P("member", "lon", None, None, None),
        P("member", "lon", None, None, None),
    )
    return jax.shard_map(
        shards, mesh=mesh, in_specs=placed, out_specs=P("member", "lon", None), check_vma=False
    )
```

```python
import functools

import jax
import jax.numpy as jnp
from jax import lax
from jax.experimental import pallas as pl
from jax.experimental.pallas import tpu as pltpu
from jax.sharding import PartitionSpec as P

TILE_CELLS = 128


gelu_coef = 0.044715
root_two_pi = 0.7978845608028654
eps_norm = 1e-06
TAPS = 7
REACH = 3
VMEM_LIMIT = 56 * 1024 * 1024


def edges(cells):
    count = lax.axis_size("lon")
    west = lax.ppermute(cells[-REACH:], "lon", [(i, (i + 1) % count) for i in range(count)])
    east = lax.ppermute(cells[:REACH], "lon", [((i + 1) % count, i) for i in range(count)])
    return west, east


def exchange(mid_ref, west_ref, east_ref, send_sem, recv_sem):
    lon_rows = mid_ref.shape[0]
    count = lax.axis_size("lon")
    here = lax.axis_index("lon")
    ahead, behind = lax.rem(here + 1, count), lax.rem(here + count - 1, count)
    barrier = pltpu.get_barrier_semaphore()
    for neighbour in (behind, ahead):
        pl.semaphore_signal(
            barrier,
            inc=1,
            device_id={"lon": neighbour},
            device_id_type=pl.DeviceIdType.MESH,
        )
    pl.semaphore_wait(barrier, 2)
    copies = []
    for at, (source, target, neighbour) in enumerate(
        (
            (mid_ref.at[pl.ds(lon_rows - REACH, REACH)], west_ref, ahead),
            (mid_ref.at[pl.ds(0, REACH)], east_ref, behind),
        )
    ):
        copy = pltpu.make_async_remote_copy(
            src_ref=source,
            dst_ref=target,
            send_sem=send_sem.at[at],
            recv_sem=recv_sem.at[at],
            device_id={"lon": neighbour},
            device_id_type=pl.DeviceIdType.MESH,
        )
        copy.start()
        copies.append(copy)
    return copies


def put_row(pad_ref, row, ref, at):
    lat_cols, hidden = ref.shape[1:]
    zeros = jnp.zeros((8, 128), jnp.float32)
    for h in range(hidden // 128):
        pad_ref[h, row, 0:8, :] = zeros
        pad_ref[h, row, 8 + lat_cols : 16 + lat_cols, :] = zeros
        pad_ref[h, row, 8 : 8 + lat_cols, :] = ref[at, :, h * 128 : (h + 1) * 128].astype(
            jnp.float32
        )


def conv_block(pad_ref, kern_ref, mix_ref, lat_start, wanted, flip):
    halves, lon_pad, _, _ = pad_ref.shape
    last = TAPS * TAPS - 1

    def piece(step, carry):
        h, sub = step // 2, step % 2
        base = pl.multiple_of(lat_start + sub * 8, 8)
        sums = {}
        for j in range(TAPS):
            taps = [i * TAPS + j for i in range(TAPS)]
            weight = [kern_ref[h, last - tap if flip else tap] for tap in taps]
            for row in range(lon_pad):
                users = [(i, row - i) for i in range(TAPS) if row - i in wanted]
                if not users:
                    continue
                cells = pad_ref[h, row, pl.ds(base + j + 8 - REACH, 8), :]
                for i, o in users:
                    term = weight[i] * cells
                    sums[o] = sums[o] + term if o in sums else term
        for o in wanted:
            mix_ref[h, o, pl.ds(pl.multiple_of(sub * 8, 8), 8), :] = sums[o]
        return carry

    lax.fori_loop(0, halves * 2, piece, 0)


def conv_all(mid_ref, kern_ref, pad_ref, mix_ref, west_ref, east_ref, sems, flip, finish):
    lon_rows, lat_cols, _ = mid_ref.shape
    copies = exchange(mid_ref, west_ref, east_ref, *sems) if sems else []
    early = lat_cols // 64 if sems else 0

    def middle_row(row, carry):
        put_row(pad_ref, row + REACH, mid_ref, row)
        return carry

    lax.fori_loop(0, lon_rows, middle_row, 0)
    inner = tuple(range(REACH, lon_rows - REACH))
    outer = tuple(o for o in range(lon_rows) if o not in inner)
    blocks = lat_cols // 16

    def run(first, end, wanted):
        def block(at, carry):
            lat = pl.multiple_of(at * 16, 16)
            conv_block(pad_ref, kern_ref, mix_ref, lat, wanted, flip)
            for o in wanted:
                halves = [mix_ref[h, o] for h in range(mix_ref.shape[0])]
                finish(o, lat, jnp.concatenate(halves, axis=1))
            return carry

        lax.fori_loop(first, end, block, 0)

    if early:
        run(0, early, inner)
    for copy in copies:
        copy.wait()
    for row in range(REACH):
        put_row(pad_ref, row, west_ref, row)
        put_row(pad_ref, lon_rows + REACH + row, east_ref, row)
    if early:
        run(0, early, outer)
    run(early, blocks, tuple(range(lon_rows)))


def conv_norm_kernel(
    mid_ref,
    kern_ref,
    gain_ref,
    normal_ref,
    normed_ref,
    inverse_ref,
    pad_ref,
    mix_ref,
    west_ref,
    east_ref,
    *sems,
):
    def finish(o, lat, mixed):
        center = mixed - jnp.mean(mixed, axis=1, keepdims=True)
        inverse = lax.rsqrt(jnp.mean(center * center, axis=1, keepdims=True) + eps_norm)
        normal = center * inverse
        normal_ref[o, pl.ds(lat, 16), :] = normal.astype(jnp.bfloat16)
        normed_ref[o, pl.ds(lat, 16), :] = (normal * gain_ref[...]).astype(jnp.bfloat16)
        inverse_ref[o, pl.ds(lat, 16), :] = jnp.broadcast_to(inverse, (16, 128))

    conv_all(mid_ref, kern_ref, pad_ref, mix_ref, west_ref, east_ref, sems, False, finish)


def conv_norm_given_kernel(west_ref, east_ref, *refs):
    conv_norm_kernel(*refs, west_ref, east_ref)


def conv_add_kernel(
    mid_ref, kern_ref, add_ref, out_ref, pad_ref, mix_ref, west_ref, east_ref, *sems
):
    def finish(o, lat, summed):
        total = add_ref[o, pl.ds(lat, 16), :].astype(jnp.float32) + summed
        out_ref[o, pl.ds(lat, 16), :] = total.astype(jnp.bfloat16)

    conv_all(mid_ref, kern_ref, pad_ref, mix_ref, west_ref, east_ref, sems, True, finish)


def conv_scratch(shape):
    lon_rows, lat_cols, hidden = shape
    halves = hidden // 128
    return [
        pltpu.VMEM((halves, lon_rows + 2 * REACH, lat_cols + 16, 128), jnp.float32),
        pltpu.VMEM((halves, lon_rows, 16, 128), jnp.float32),
        pltpu.VMEM((REACH, lat_cols, hidden), jnp.bfloat16),
        pltpu.VMEM((REACH, lat_cols, hidden), jnp.bfloat16),
        pltpu.SemaphoreType.DMA((2,)),
        pltpu.SemaphoreType.DMA((2,)),
    ]


def conv_cost(shape):
    cells = shape[0] * shape[1] * shape[2]
    return pl.CostEstimate(flops=cells * 98, bytes_accessed=cells * 12, transcendentals=0)


def in_vmem(count):
    return [pl.BlockSpec(memory_space=pltpu.VMEM)] * count


def conv_norm(cells, kern, gain, given):
    shape = cells.shape
    return pl.pallas_call(
        conv_norm_given_kernel if given else conv_norm_kernel,
        out_shape=(
            jax.ShapeDtypeStruct(shape, jnp.bfloat16),
            jax.ShapeDtypeStruct(shape, jnp.bfloat16),
            jax.ShapeDtypeStruct(shape[:2] + (128,), jnp.float32),
        ),
        in_specs=in_vmem(5 if given else 3),
        out_specs=tuple(in_vmem(3)),
        scratch_shapes=conv_scratch(shape)[: 2 if given else None],
        cost_estimate=conv_cost(shape),
        compiler_params=pltpu.CompilerParams(vmem_limit_bytes=VMEM_LIMIT)
        if given
        else pltpu.CompilerParams(
            vmem_limit_bytes=VMEM_LIMIT, collective_id=0, has_side_effects=True
        ),
    )(*(edges(cells) if given else ()), cells, kern, gain)


def conv_add(cells, kern, add):
    shape = cells.shape
    return pl.pallas_call(
        conv_add_kernel,
        out_shape=jax.ShapeDtypeStruct(shape, jnp.bfloat16),
        in_specs=in_vmem(3),
        out_specs=pl.BlockSpec(memory_space=pltpu.VMEM),
        scratch_shapes=conv_scratch(shape),
        cost_estimate=conv_cost(shape),
        compiler_params=pltpu.CompilerParams(
            vmem_limit_bytes=VMEM_LIMIT, collective_id=1, has_side_effects=True
        ),
    )(cells, kern, add)


def mlp_kernel(piece, normed_ref, lifted_ref, up_ref, down_ref, block_ref, slope_ref):
    normed = normed_ref[...]
    total = lifted_ref[...].astype(jnp.float32)
    for start in range(0, up_ref.shape[1], piece):
        z = jnp.dot(normed, up_ref[:, start : start + piece], preferred_element_type=jnp.float32)
        square = z * z
        tanh_val = jnp.tanh(z * (root_two_pi + root_two_pi * gelu_coef * square))
        half = 0.5 + 0.5 * tanh_val
        active = (z * half).astype(jnp.bfloat16)
        bend = z * (root_two_pi + 3.0 * root_two_pi * gelu_coef * square)
        slope = half + half * (1.0 - tanh_val) * bend
        slope_ref[:, start : start + piece] = slope.astype(jnp.bfloat16)
        total = total + jnp.dot(
            active, down_ref[start : start + piece, :], preferred_element_type=jnp.float32
        )
    block_ref[...] = total.astype(jnp.bfloat16)


def mlp(normed, lifted, up_weight, down_weight, rows=512, piece=256):
    amount, hidden = normed.shape
    wide = up_weight.shape[1]
    by_rows = lambda width: pl.BlockSpec((rows, width), lambda r: (r, 0))
    whole = lambda shape: pl.BlockSpec(shape, lambda r: (0, 0))
    return pl.pallas_call(
        functools.partial(mlp_kernel, piece),
        grid=(amount // rows,),
        out_shape=(
            jax.ShapeDtypeStruct((amount, hidden), jnp.bfloat16),
            jax.ShapeDtypeStruct((amount, wide), jnp.bfloat16),
        ),
        in_specs=[by_rows(hidden), by_rows(hidden), whole((hidden, wide)), whole((wide, hidden))],
        out_specs=(by_rows(hidden), by_rows(wide)),
        cost_estimate=pl.CostEstimate(
            flops=4 * amount * hidden * wide,
            bytes_accessed=amount * (wide + 3 * hidden) * 2,
            transcendentals=amount * wide,
        ),
        compiler_params=pltpu.CompilerParams(vmem_limit_bytes=VMEM_LIMIT),
    )(normed, lifted, up_weight, down_weight)


def mlp_back_kernel(
    piece, block_ref, slope_ref, normal_ref, inverse_ref, gain_ref, up_ref, down_ref, out_ref
):
    g_block = block_ref[...]
    across = (((1,), (1,)), ((), ()))
    total = None
    for start in range(0, up_ref.shape[1], piece):
        g_active = lax.dot_general(
            g_block,
            down_ref[start : start + piece, :],
            across,
            preferred_element_type=jnp.float32,
        )
        g_middle = g_active * slope_ref[:, start : start + piece].astype(jnp.float32)
        term = lax.dot_general(
            g_middle.astype(jnp.bfloat16),
            up_ref[:, start : start + piece],
            across,
            preferred_element_type=jnp.float32,
        )
        total = term if total is None else total + term
    g_scaled = total * gain_ref[...]
    normal = normal_ref[...].astype(jnp.float32)
    g_mixed = inverse_ref[:, 0:1] * (
        g_scaled
        - jnp.mean(g_scaled, axis=1, keepdims=True)
        - normal * jnp.mean(g_scaled * normal, axis=1, keepdims=True)
    )
    out_ref[...] = g_mixed.astype(jnp.bfloat16)


def mlp_back(g_block, slope, normal, inverse, gain, up_weight, down_weight, rows=512, piece=256):
    amount, hidden = g_block.shape
    wide = up_weight.shape[1]
    by_rows = lambda width: pl.BlockSpec((rows, width), lambda r: (r, 0))
    whole = lambda shape: pl.BlockSpec(shape, lambda r: (0, 0))
    return pl.pallas_call(
        functools.partial(mlp_back_kernel, piece),
        grid=(amount // rows,),
        out_shape=jax.ShapeDtypeStruct((amount, hidden), jnp.bfloat16),
        in_specs=[
            by_rows(hidden),
            by_rows(wide),
            by_rows(hidden),
            by_rows(128),
            whole((1, hidden)),
            whole((hidden, wide)),
            whole((wide, hidden)),
        ],
        out_specs=by_rows(hidden),
        cost_estimate=pl.CostEstimate(
            flops=4 * amount * hidden * wide,
            bytes_accessed=amount * (2 * wide + 8 * hidden),
            transcendentals=0,
        ),
        compiler_params=pltpu.CompilerParams(vmem_limit_bytes=VMEM_LIMIT),
    )(g_block, slope, normal, inverse, gain, up_weight, down_weight)


def forward_step(state_field, weights, given):
    lift_weight, kern, gain, up_weight, down_weight, out_weight = weights
    channels, lon_rows, lat_cols = state_field.shape
    hidden = lift_weight.shape[1]
    lifted = lax.dot_general(
        state_field.astype(jnp.bfloat16),
        lift_weight,
        (((0,), (0,)), ((), ())),
        preferred_element_type=jnp.float32,
    ).astype(jnp.bfloat16)
    normal, normed, inverse = conv_norm(lifted, kern, gain, given)
    block_out, slope = mlp(
        normed.reshape(-1, hidden), lifted.reshape(-1, hidden), up_weight, down_weight
    )
    change = lax.dot_general(
        out_weight, block_out, (((0,), (1,)), ((), ())), preferred_element_type=jnp.float32
    )
    saved = (normal.reshape(-1, hidden), inverse.reshape(-1, 128), slope)
    return state_field + change.reshape(channels, lon_rows, lat_cols), saved


def backward_step(cotangent, saved, weights):
    lift_weight, kern, gain, up_weight, down_weight, out_weight = weights
    normal, inverse, slope = saved
    channels, lon_rows, lat_cols = cotangent.shape
    hidden = lift_weight.shape[1]
    g_block = lax.dot_general(
        cotangent.astype(jnp.bfloat16),
        out_weight,
        (((0,), (1,)), ((), ())),
        preferred_element_type=jnp.float32,
    ).astype(jnp.bfloat16)
    g_mixed = mlp_back(
        g_block.reshape(-1, hidden), slope, normal, inverse, gain, up_weight, down_weight
    ).reshape(lon_rows, lat_cols, hidden)
    g_lifted = conv_add(g_mixed, kern, g_block)
    g_state = lax.dot_general(
        lift_weight, g_lifted, (((1,), (2,)), ((), ())), preferred_element_type=jnp.float32
    )
    return cotangent + g_state


def tile_ops(cell_ids, point_weights):
    positions = jnp.arange(TILE_CELLS, dtype=jnp.int32)
    return jnp.sum(
        point_weights[..., None] * (cell_ids[..., None] == positions).astype(jnp.float32), axis=2
    )


def to_tiles(state_field):
    channels, lon_rows, lat_cols = state_field.shape
    tile_rows = TILE_CELLS // lon_rows
    split = state_field.reshape(channels, lon_rows, lat_cols // tile_rows, tile_rows)
    return split.transpose(2, 0, 1, 3).reshape(lat_cols // tile_rows, channels, TILE_CELLS)


def from_tiles(tile_sums, lon_rows):
    tile_total, channels, _ = tile_sums.shape
    tile_rows = TILE_CELLS // lon_rows
    split = tile_sums.reshape(tile_total, channels, lon_rows, tile_rows)
    return split.transpose(1, 2, 0, 3).reshape(channels, lon_rows, tile_total * tile_rows)


def slot_selector(owner_ids, band_count, place_count):
    hit = owner_ids[:, None] == jnp.arange(band_count, dtype=jnp.int32)[None, :]
    slots = jnp.arange(owner_ids.shape[0], dtype=jnp.int32)
    earlier = (slots[None, :] < slots[:, None]).astype(jnp.bfloat16)
    before = jnp.dot(earlier, hit.astype(jnp.bfloat16), preferred_element_type=jnp.float32)
    place = jnp.sum(jnp.where(hit, before, 0.0), axis=1).astype(jnp.int32)
    slot_code = owner_ids * place_count + place
    return (
        slot_code[:, None] == jnp.arange(band_count * place_count, dtype=jnp.int32)[None, :]
    ).astype(jnp.bfloat16)


def owners_data(obs_values, obs_precision):
    channels = obs_values.shape[-1]
    widen = ((0, 0), (0, 0), (0, 0), (0, 128 - channels))
    both = jnp.concatenate(
        [jnp.pad(part[:, 0].astype(jnp.bfloat16), widen) for part in (obs_values, obs_precision)],
        axis=3,
    ).transpose(1, 0, 2, 3)
    return lax.all_to_all(both, "lon", split_axis=0, concat_axis=0, tiled=True)


def shards(
    state_start,
    lift_weight,
    conv_kernel,
    norm_gain,
    up_weight,
    down_weight,
    out_weight,
    obs_cells,
    obs_weights,
    tile_counts,
    obs_owner,
    obs_values,
    obs_precision,
):
    hidden = norm_gain.shape[0]
    by_half = lambda taps: jnp.broadcast_to(
        taps.reshape(-1, 1, hidden // 128, 128).transpose(2, 0, 1, 3),
        (hidden // 128, taps.shape[0], 8, 128),
    )
    weights = (
        lift_weight,
        by_half(conv_kernel),
        norm_gain.reshape(1, hidden),
        up_weight,
        down_weight,
        out_weight,
    )
    channels, lon_rows = (state_start.shape[0], state_start.shape[1])
    band_count, place_count = (obs_values.shape[2], obs_values.shape[3])
    tile_total, slot_total = (obs_cells.shape[1], obs_cells.shape[2])
    arrived = owners_data(obs_values, obs_precision)
    operators = [
        tile_ops(obs_cells[moment], obs_weights[moment]).astype(jnp.bfloat16) for moment in range(2)
    ]
    state_one, saved_zero = forward_step(state_start, weights, True)
    state_two, saved_one = forward_step(state_one, weights, False)

    def pulled(moment, state_field):
        selector = slot_selector(obs_owner[moment, :, 0], band_count, place_count)
        chosen = jnp.dot(
            selector,
            arrived[:, moment].reshape(band_count * place_count, -1),
            preferred_element_type=jnp.float32,
        )
        live_slots = (
            (jnp.arange(slot_total, dtype=jnp.int32)[None, :] < tile_counts[moment][:, None])
            .astype(jnp.float32)
            .reshape(-1, 1)
        )
        model_equiv = jnp.einsum(
            "gkc,gsc->gks",
            operators[moment],
            to_tiles(state_field.astype(jnp.bfloat16)),
            preferred_element_type=jnp.float32,
        ).reshape(-1, channels)
        misfit = live_slots * (
            chosen[:, 128 : 128 + channels] * (model_equiv - chosen[:, :channels])
        )
        tile_sums = jnp.einsum(
            "gkc,gks->gsc",
            operators[moment],
            misfit.reshape(tile_total, slot_total, channels).astype(jnp.bfloat16),
            preferred_element_type=jnp.float32,
        )
        return from_tiles(tile_sums, lon_rows)

    carried = backward_step(pulled(1, state_two), saved_one, weights) + pulled(0, state_one)
    return backward_step(carried, saved_zero, weights)


def solution(mesh):
    placed = (
        P("member", "lon", None),
        P(),
        P(),
        P(),
        P(),
        P(),
        P(),
        P("member", "lon", None, None),
        P("member", "lon", None, None),
        P("member", "lon"),
        P("member", "lon", None),
        P("member", "lon", None, None, None),
        P("member", "lon", None, None, None),
    )
    return jax.shard_map(
        shards, mesh=mesh, in_specs=placed, out_specs=P("member", "lon", None), check_vma=False
    )
```

```python
import functools

import jax
import jax.numpy as jnp
from jax import lax
from jax.experimental import pallas as pl
from jax.experimental.pallas import tpu as pltpu
from jax.sharding import PartitionSpec as P

TILE_CELLS = 128


gelu_coef = 0.044715
root_two_pi = 0.7978845608028654
eps_norm = 1e-06
TAPS = 7
REACH = 3
VMEM_LIMIT = 56 * 1024 * 1024


def edges(cells):
    count = lax.axis_size("lon")
    west = lax.ppermute(cells[-REACH:], "lon", [(i, (i + 1) % count) for i in range(count)])
    east = lax.ppermute(cells[:REACH], "lon", [((i + 1) % count, i) for i in range(count)])
    return west, east


def exchange(mid_ref, west_ref, east_ref, send_sem, recv_sem):
    lon_rows = mid_ref.shape[0]
    count = lax.axis_size("lon")
    here = lax.axis_index("lon")
    ahead, behind = lax.rem(here + 1, count), lax.rem(here + count - 1, count)
    barrier = pltpu.get_barrier_semaphore()
    for neighbour in (behind, ahead):
        pl.semaphore_signal(
            barrier,
            inc=1,
            device_id={"lon": neighbour},
            device_id_type=pl.DeviceIdType.MESH,
        )
    pl.semaphore_wait(barrier, 2)
    copies = []
    for at, (source, target, neighbour) in enumerate(
        (
            (mid_ref.at[pl.ds(lon_rows - REACH, REACH)], west_ref, ahead),
            (mid_ref.at[pl.ds(0, REACH)], east_ref, behind),
        )
    ):
        copy = pltpu.make_async_remote_copy(
            src_ref=source,
            dst_ref=target,
            send_sem=send_sem.at[at],
            recv_sem=recv_sem.at[at],
            device_id={"lon": neighbour},
            device_id_type=pl.DeviceIdType.MESH,
        )
        copy.start()
        copies.append(copy)
    return copies


def put_row(pad_ref, row, ref, at):
    lat_cols, hidden = ref.shape[1:]
    zeros = jnp.zeros((8, 128), jnp.float32)
    for h in range(hidden // 128):
        pad_ref[h, row, 0:8, :] = zeros
        pad_ref[h, row, 8 + lat_cols : 16 + lat_cols, :] = zeros
        pad_ref[h, row, 8 : 8 + lat_cols, :] = ref[at, :, h * 128 : (h + 1) * 128].astype(
            jnp.float32
        )


def conv_block(pad_ref, kern_ref, mix_ref, lat_start, wanted, flip):
    halves, lon_pad, _, _ = pad_ref.shape
    last = TAPS * TAPS - 1

    def piece(step, carry):
        h, sub = step // 2, step % 2
        base = pl.multiple_of(lat_start + sub * 8, 8)
        sums = {}
        for j in range(TAPS):
            taps = [i * TAPS + j for i in range(TAPS)]
            weight = [kern_ref[h, last - tap if flip else tap] for tap in taps]
            for row in range(lon_pad):
                users = [(i, row - i) for i in range(TAPS) if row - i in wanted]
                if not users:
                    continue
                cells = pad_ref[h, row, pl.ds(base + j + 8 - REACH, 8), :]
                for i, o in users:
                    term = weight[i] * cells
                    sums[o] = sums[o] + term if o in sums else term
        for o in wanted:
            mix_ref[h, o, pl.ds(pl.multiple_of(sub * 8, 8), 8), :] = sums[o]
        return carry

    lax.fori_loop(0, halves * 2, piece, 0)


def conv_all(mid_ref, kern_ref, pad_ref, mix_ref, west_ref, east_ref, sems, flip, finish):
    lon_rows, lat_cols, _ = mid_ref.shape
    copies = exchange(mid_ref, west_ref, east_ref, *sems) if sems else []
    early = 3 * lat_cols // 64 if sems else 0

    def middle_row(row, carry):
        put_row(pad_ref, row + REACH, mid_ref, row)
        return carry

    lax.fori_loop(0, lon_rows, middle_row, 0)
    inner = tuple(range(REACH, lon_rows - REACH))
    outer = tuple(o for o in range(lon_rows) if o not in inner)
    blocks = lat_cols // 16

    def run(first, end, wanted):
        def block(at, carry):
            lat = pl.multiple_of(at * 16, 16)
            conv_block(pad_ref, kern_ref, mix_ref, lat, wanted, flip)
            for o in wanted:
                halves = [mix_ref[h, o] for h in range(mix_ref.shape[0])]
                finish(o, lat, jnp.concatenate(halves, axis=1))
            return carry

        lax.fori_loop(first, end, block, 0)

    if early:
        run(0, early, inner)
    for copy in copies:
        copy.wait()
    for row in range(REACH):
        put_row(pad_ref, row, west_ref, row)
        put_row(pad_ref, lon_rows + REACH + row, east_ref, row)
    if early:
        run(0, early, outer)
    run(early, blocks, tuple(range(lon_rows)))


def conv_norm_kernel(
    mid_ref,
    kern_ref,
    gain_ref,
    normal_ref,
    normed_ref,
    inverse_ref,
    pad_ref,
    mix_ref,
    west_ref,
    east_ref,
    *sems,
):
    def finish(o, lat, mixed):
        center = mixed - jnp.mean(mixed, axis=1, keepdims=True)
        inverse = lax.rsqrt(jnp.mean(center * center, axis=1, keepdims=True) + eps_norm)
        normal = center * inverse
        normal_ref[o, pl.ds(lat, 16), :] = normal.astype(jnp.bfloat16)
        normed_ref[o, pl.ds(lat, 16), :] = (normal * gain_ref[...]).astype(jnp.bfloat16)
        inverse_ref[o, pl.ds(lat, 16), :] = jnp.broadcast_to(inverse, (16, 128))

    conv_all(mid_ref, kern_ref, pad_ref, mix_ref, west_ref, east_ref, sems, False, finish)


def conv_norm_given_kernel(west_ref, east_ref, *refs):
    conv_norm_kernel(*refs, west_ref, east_ref)


def conv_add_kernel(
    mid_ref, kern_ref, add_ref, out_ref, pad_ref, mix_ref, west_ref, east_ref, *sems
):
    def finish(o, lat, summed):
        total = add_ref[o, pl.ds(lat, 16), :].astype(jnp.float32) + summed
        out_ref[o, pl.ds(lat, 16), :] = total.astype(jnp.bfloat16)

    conv_all(mid_ref, kern_ref, pad_ref, mix_ref, west_ref, east_ref, sems, True, finish)


def conv_scratch(shape):
    lon_rows, lat_cols, hidden = shape
    halves = hidden // 128
    return [
        pltpu.VMEM((halves, lon_rows + 2 * REACH, lat_cols + 16, 128), jnp.float32),
        pltpu.VMEM((halves, lon_rows, 16, 128), jnp.float32),
        pltpu.VMEM((REACH, lat_cols, hidden), jnp.bfloat16),
        pltpu.VMEM((REACH, lat_cols, hidden), jnp.bfloat16),
        pltpu.SemaphoreType.DMA((2,)),
        pltpu.SemaphoreType.DMA((2,)),
    ]


def conv_cost(shape):
    cells = shape[0] * shape[1] * shape[2]
    return pl.CostEstimate(flops=cells * 98, bytes_accessed=cells * 12, transcendentals=0)


def in_vmem(count):
    return [pl.BlockSpec(memory_space=pltpu.VMEM)] * count


def conv_norm(cells, kern, gain, given):
    shape = cells.shape
    return pl.pallas_call(
        conv_norm_given_kernel if given else conv_norm_kernel,
        out_shape=(
            jax.ShapeDtypeStruct(shape, jnp.bfloat16),
            jax.ShapeDtypeStruct(shape, jnp.bfloat16),
            jax.ShapeDtypeStruct(shape[:2] + (128,), jnp.float32),
        ),
        in_specs=in_vmem(5 if given else 3),
        out_specs=tuple(in_vmem(3)),
        scratch_shapes=conv_scratch(shape)[: 2 if given else None],
        cost_estimate=conv_cost(shape),
        compiler_params=pltpu.CompilerParams(vmem_limit_bytes=VMEM_LIMIT)
        if given
        else pltpu.CompilerParams(
            vmem_limit_bytes=VMEM_LIMIT, collective_id=0, has_side_effects=True
        ),
    )(*(edges(cells) if given else ()), cells, kern, gain)


def conv_add(cells, kern, add):
    shape = cells.shape
    return pl.pallas_call(
        conv_add_kernel,
        out_shape=jax.ShapeDtypeStruct(shape, jnp.bfloat16),
        in_specs=in_vmem(3),
        out_specs=pl.BlockSpec(memory_space=pltpu.VMEM),
        scratch_shapes=conv_scratch(shape),
        cost_estimate=conv_cost(shape),
        compiler_params=pltpu.CompilerParams(
            vmem_limit_bytes=VMEM_LIMIT, collective_id=1, has_side_effects=True
        ),
    )(cells, kern, add)


def mlp_kernel(piece, normed_ref, lifted_ref, up_ref, down_ref, block_ref, slope_ref):
    normed = normed_ref[...]
    total = lifted_ref[...].astype(jnp.float32)
    for start in range(0, up_ref.shape[1], piece):
        z = jnp.dot(normed, up_ref[:, start : start + piece], preferred_element_type=jnp.float32)
        square = z * z
        tanh_val = jnp.tanh(z * (root_two_pi + root_two_pi * gelu_coef * square))
        half = 0.5 + 0.5 * tanh_val
        active = (z * half).astype(jnp.bfloat16)
        bend = z * (root_two_pi + 3.0 * root_two_pi * gelu_coef * square)
        slope = half + half * (1.0 - tanh_val) * bend
        slope_ref[:, start : start + piece] = slope.astype(jnp.bfloat16)
        total = total + jnp.dot(
            active, down_ref[start : start + piece, :], preferred_element_type=jnp.float32
        )
    block_ref[...] = total.astype(jnp.bfloat16)


def mlp(normed, lifted, up_weight, down_weight, rows=512, piece=256):
    amount, hidden = normed.shape
    wide = up_weight.shape[1]
    by_rows = lambda width: pl.BlockSpec((rows, width), lambda r: (r, 0))
    whole = lambda shape: pl.BlockSpec(shape, lambda r: (0, 0))
    return pl.pallas_call(
        functools.partial(mlp_kernel, piece),
        grid=(amount // rows,),
        out_shape=(
            jax.ShapeDtypeStruct((amount, hidden), jnp.bfloat16),
            jax.ShapeDtypeStruct((amount, wide), jnp.bfloat16),
        ),
        in_specs=[by_rows(hidden), by_rows(hidden), whole((hidden, wide)), whole((wide, hidden))],
        out_specs=(by_rows(hidden), by_rows(wide)),
        cost_estimate=pl.CostEstimate(
            flops=4 * amount * hidden * wide,
            bytes_accessed=amount * (wide + 3 * hidden) * 2,
            transcendentals=amount * wide,
        ),
        compiler_params=pltpu.CompilerParams(vmem_limit_bytes=VMEM_LIMIT),
    )(normed, lifted, up_weight, down_weight)


def mlp_back_kernel(
    piece, block_ref, slope_ref, normal_ref, inverse_ref, gain_ref, up_ref, down_ref, out_ref
):
    g_block = block_ref[...]
    across = (((1,), (1,)), ((), ()))
    total = None
    for start in range(0, up_ref.shape[1], piece):
        g_active = lax.dot_general(
            g_block,
            down_ref[start : start + piece, :],
            across,
            preferred_element_type=jnp.float32,
        )
        g_middle = g_active * slope_ref[:, start : start + piece].astype(jnp.float32)
        term = lax.dot_general(
            g_middle.astype(jnp.bfloat16),
            up_ref[:, start : start + piece],
            across,
            preferred_element_type=jnp.float32,
        )
        total = term if total is None else total + term
    g_scaled = total * gain_ref[...]
    normal = normal_ref[...].astype(jnp.float32)
    g_mixed = inverse_ref[:, 0:1] * (
        g_scaled
        - jnp.mean(g_scaled, axis=1, keepdims=True)
        - normal * jnp.mean(g_scaled * normal, axis=1, keepdims=True)
    )
    out_ref[...] = g_mixed.astype(jnp.bfloat16)


def mlp_back(g_block, slope, normal, inverse, gain, up_weight, down_weight, rows=512, piece=256):
    amount, hidden = g_block.shape
    wide = up_weight.shape[1]
    by_rows = lambda width: pl.BlockSpec((rows, width), lambda r: (r, 0))
    whole = lambda shape: pl.BlockSpec(shape, lambda r: (0, 0))
    return pl.pallas_call(
        functools.partial(mlp_back_kernel, piece),
        grid=(amount // rows,),
        out_shape=jax.ShapeDtypeStruct((amount, hidden), jnp.bfloat16),
        in_specs=[
            by_rows(hidden),
            by_rows(wide),
            by_rows(hidden),
            by_rows(128),
            whole((1, hidden)),
            whole((hidden, wide)),
            whole((wide, hidden)),
        ],
        out_specs=by_rows(hidden),
        cost_estimate=pl.CostEstimate(
            flops=4 * amount * hidden * wide,
            bytes_accessed=amount * (2 * wide + 8 * hidden),
            transcendentals=0,
        ),
        compiler_params=pltpu.CompilerParams(vmem_limit_bytes=VMEM_LIMIT),
    )(g_block, slope, normal, inverse, gain, up_weight, down_weight)


def forward_step(state_field, weights, given):
    lift_weight, kern, gain, up_weight, down_weight, out_weight = weights
    channels, lon_rows, lat_cols = state_field.shape
    hidden = lift_weight.shape[1]
    lifted = lax.dot_general(
        state_field.astype(jnp.bfloat16),
        lift_weight,
        (((0,), (0,)), ((), ())),
        preferred_element_type=jnp.float32,
    ).astype(jnp.bfloat16)
    normal, normed, inverse = conv_norm(lifted, kern, gain, given)
    block_out, slope = mlp(
        normed.reshape(-1, hidden), lifted.reshape(-1, hidden), up_weight, down_weight
    )
    change = lax.dot_general(
        out_weight, block_out, (((0,), (1,)), ((), ())), preferred_element_type=jnp.float32
    )
    saved = (normal.reshape(-1, hidden), inverse.reshape(-1, 128), slope)
    return state_field + change.reshape(channels, lon_rows, lat_cols), saved


def backward_step(cotangent, saved, weights):
    lift_weight, kern, gain, up_weight, down_weight, out_weight = weights
    normal, inverse, slope = saved
    channels, lon_rows, lat_cols = cotangent.shape
    hidden = lift_weight.shape[1]
    g_block = lax.dot_general(
        cotangent.astype(jnp.bfloat16),
        out_weight,
        (((0,), (1,)), ((), ())),
        preferred_element_type=jnp.float32,
    ).astype(jnp.bfloat16)
    g_mixed = mlp_back(
        g_block.reshape(-1, hidden), slope, normal, inverse, gain, up_weight, down_weight
    ).reshape(lon_rows, lat_cols, hidden)
    g_lifted = conv_add(g_mixed, kern, g_block)
    g_state = lax.dot_general(
        lift_weight, g_lifted, (((1,), (2,)), ((), ())), preferred_element_type=jnp.float32
    )
    return cotangent + g_state


def tile_ops(cell_ids, point_weights):
    positions = jnp.arange(TILE_CELLS, dtype=jnp.int32)
    return jnp.sum(
        point_weights[..., None] * (cell_ids[..., None] == positions).astype(jnp.float32), axis=2
    )


def to_tiles(state_field):
    channels, lon_rows, lat_cols = state_field.shape
    tile_rows = TILE_CELLS // lon_rows
    split = state_field.reshape(channels, lon_rows, lat_cols // tile_rows, tile_rows)
    return split.transpose(2, 0, 1, 3).reshape(lat_cols // tile_rows, channels, TILE_CELLS)


def from_tiles(tile_sums, lon_rows):
    tile_total, channels, _ = tile_sums.shape
    tile_rows = TILE_CELLS // lon_rows
    split = tile_sums.reshape(tile_total, channels, lon_rows, tile_rows)
    return split.transpose(1, 2, 0, 3).reshape(channels, lon_rows, tile_total * tile_rows)


def slot_selector(owner_ids, band_count, place_count):
    hit = owner_ids[:, None] == jnp.arange(band_count, dtype=jnp.int32)[None, :]
    slots = jnp.arange(owner_ids.shape[0], dtype=jnp.int32)
    earlier = (slots[None, :] < slots[:, None]).astype(jnp.bfloat16)
    before = jnp.dot(earlier, hit.astype(jnp.bfloat16), preferred_element_type=jnp.float32)
    place = jnp.sum(jnp.where(hit, before, 0.0), axis=1).astype(jnp.int32)
    slot_code = owner_ids * place_count + place
    return (
        slot_code[:, None] == jnp.arange(band_count * place_count, dtype=jnp.int32)[None, :]
    ).astype(jnp.bfloat16)


def owners_data(obs_values, obs_precision):
    channels = obs_values.shape[-1]
    widen = ((0, 0), (0, 0), (0, 0), (0, 128 - channels))
    both = jnp.concatenate(
        [jnp.pad(part[:, 0].astype(jnp.bfloat16), widen) for part in (obs_values, obs_precision)],
        axis=3,
    ).transpose(1, 0, 2, 3)
    return lax.all_to_all(both, "lon", split_axis=0, concat_axis=0, tiled=True)


def shards(
    state_start,
    lift_weight,
    conv_kernel,
    norm_gain,
    up_weight,
    down_weight,
    out_weight,
    obs_cells,
    obs_weights,
    tile_counts,
    obs_owner,
    obs_values,
    obs_precision,
):
    hidden = norm_gain.shape[0]
    by_half = lambda taps: jnp.broadcast_to(
        taps.reshape(-1, 1, hidden // 128, 128).transpose(2, 0, 1, 3),
        (hidden // 128, taps.shape[0], 8, 128),
    )
    weights = (
        lift_weight,
        by_half(conv_kernel),
        norm_gain.reshape(1, hidden),
        up_weight,
        down_weight,
        out_weight,
    )
    channels, lon_rows = (state_start.shape[0], state_start.shape[1])
    band_count, place_count = (obs_values.shape[2], obs_values.shape[3])
    tile_total, slot_total = (obs_cells.shape[1], obs_cells.shape[2])
    arrived = owners_data(obs_values, obs_precision)
    operators = [
        tile_ops(obs_cells[moment], obs_weights[moment]).astype(jnp.bfloat16) for moment in range(2)
    ]
    state_one, saved_zero = forward_step(state_start, weights, True)
    state_two, saved_one = forward_step(state_one, weights, False)

    def pulled(moment, state_field):
        selector = slot_selector(obs_owner[moment, :, 0], band_count, place_count)
        chosen = jnp.dot(
            selector,
            arrived[:, moment].reshape(band_count * place_count, -1),
            preferred_element_type=jnp.float32,
        )
        live_slots = (
            (jnp.arange(slot_total, dtype=jnp.int32)[None, :] < tile_counts[moment][:, None])
            .astype(jnp.float32)
            .reshape(-1, 1)
        )
        model_equiv = jnp.einsum(
            "gkc,gsc->gks",
            operators[moment],
            to_tiles(state_field.astype(jnp.bfloat16)),
            preferred_element_type=jnp.float32,
        ).reshape(-1, channels)
        misfit = live_slots * (
            chosen[:, 128 : 128 + channels] * (model_equiv - chosen[:, :channels])
        )
        tile_sums = jnp.einsum(
            "gkc,gks->gsc",
            operators[moment],
            misfit.reshape(tile_total, slot_total, channels).astype(jnp.bfloat16),
            preferred_element_type=jnp.float32,
        )
        return from_tiles(tile_sums, lon_rows)

    carried = backward_step(pulled(1, state_two), saved_one, weights) + pulled(0, state_one)
    return backward_step(carried, saved_zero, weights)


def solution(mesh):
    placed = (
        P("member", "lon", None),
        P(),
        P(),
        P(),
        P(),
        P(),
        P(),
        P("member", "lon", None, None),
        P("member", "lon", None, None),
        P("member", "lon"),
        P("member", "lon", None),
        P("member", "lon", None, None, None),
        P("member", "lon", None, None, None),
    )
    return jax.shard_map(
        shards, mesh=mesh, in_specs=placed, out_specs=P("member", "lon", None), check_vma=False
    )
```

```python
import functools

import jax
import jax.numpy as jnp
from jax import lax
from jax.experimental import pallas as pl
from jax.experimental.pallas import tpu as pltpu
from jax.sharding import PartitionSpec as P

TILE_CELLS = 128


gelu_coef = 0.044715
root_two_pi = 0.7978845608028654
eps_norm = 1e-06
TAPS = 7
REACH = 3
VMEM_LIMIT = 56 * 1024 * 1024


def edges(cells):
    count = lax.axis_size("lon")
    west = lax.ppermute(cells[-REACH:], "lon", [(i, (i + 1) % count) for i in range(count)])
    east = lax.ppermute(cells[:REACH], "lon", [((i + 1) % count, i) for i in range(count)])
    return west, east


def exchange(mid_ref, west_ref, east_ref, send_sem, recv_sem):
    lon_rows = mid_ref.shape[0]
    count = lax.axis_size("lon")
    here = lax.axis_index("lon")
    ahead, behind = lax.rem(here + 1, count), lax.rem(here + count - 1, count)
    barrier = pltpu.get_barrier_semaphore()
    for neighbour in (behind, ahead):
        pl.semaphore_signal(
            barrier,
            inc=1,
            device_id={"lon": neighbour},
            device_id_type=pl.DeviceIdType.MESH,
        )
    pl.semaphore_wait(barrier, 2)
    copies = []
    for at, (source, target, neighbour) in enumerate(
        (
            (mid_ref.at[pl.ds(lon_rows - REACH, REACH)], west_ref, ahead),
            (mid_ref.at[pl.ds(0, REACH)], east_ref, behind),
        )
    ):
        copy = pltpu.make_async_remote_copy(
            src_ref=source,
            dst_ref=target,
            send_sem=send_sem.at[at],
            recv_sem=recv_sem.at[at],
            device_id={"lon": neighbour},
            device_id_type=pl.DeviceIdType.MESH,
        )
        copy.start()
        copies.append(copy)
    return copies


def put_row(pad_ref, row, ref, at):
    lat_cols, hidden = ref.shape[1:]
    zeros = jnp.zeros((8, 128), jnp.float32)
    for h in range(hidden // 128):
        pad_ref[h, row, 0:8, :] = zeros
        pad_ref[h, row, 8 + lat_cols : 16 + lat_cols, :] = zeros
        pad_ref[h, row, 8 : 8 + lat_cols, :] = ref[at, :, h * 128 : (h + 1) * 128].astype(
            jnp.float32
        )


def conv_block(pad_ref, kern_ref, mix_ref, lat_start, wanted, flip):
    halves, lon_pad, _, _ = pad_ref.shape
    last = TAPS * TAPS - 1

    def piece(step, carry):
        h, sub = step // 2, step % 2
        base = pl.multiple_of(lat_start + sub * 8, 8)
        sums = {}
        for j in range(TAPS):
            taps = [i * TAPS + j for i in range(TAPS)]
            weight = [kern_ref[h, last - tap if flip else tap] for tap in taps]
            for row in range(lon_pad):
                users = [(i, row - i) for i in range(TAPS) if row - i in wanted]
                if not users:
                    continue
                cells = pad_ref[h, row, pl.ds(base + j + 8 - REACH, 8), :]
                for i, o in users:
                    term = weight[i] * cells
                    sums[o] = sums[o] + term if o in sums else term
        for o in wanted:
            mix_ref[h, o, pl.ds(pl.multiple_of(sub * 8, 8), 8), :] = sums[o]
        return carry

    lax.fori_loop(0, halves * 2, piece, 0)


def conv_all(mid_ref, kern_ref, pad_ref, mix_ref, west_ref, east_ref, sems, flip, finish):
    lon_rows, lat_cols, _ = mid_ref.shape
    copies = exchange(mid_ref, west_ref, east_ref, *sems) if sems else []
    early = 3 * lat_cols // 64 if sems else 0

    def middle_row(row, carry):
        put_row(pad_ref, row + REACH, mid_ref, row)
        return carry

    lax.fori_loop(0, lon_rows, middle_row, 0)
    inner = tuple(range(REACH, lon_rows - REACH))
    outer = tuple(o for o in range(lon_rows) if o not in inner)
    blocks = lat_cols // 16

    def run(first, end, wanted):
        def block(at, carry):
            lat = pl.multiple_of(at * 16, 16)
            conv_block(pad_ref, kern_ref, mix_ref, lat, wanted, flip)
            for o in wanted:
                halves = [mix_ref[h, o] for h in range(mix_ref.shape[0])]
                finish(o, lat, jnp.concatenate(halves, axis=1))
            return carry

        lax.fori_loop(first, end, block, 0)

    if early:
        run(0, early, inner)
    for copy in copies:
        copy.wait()
    for row in range(REACH):
        put_row(pad_ref, row, west_ref, row)
        put_row(pad_ref, lon_rows + REACH + row, east_ref, row)
    if early:
        run(0, early, outer)
    run(early, blocks, tuple(range(lon_rows)))


def conv_norm_kernel(
    mid_ref,
    kern_ref,
    gain_ref,
    normal_ref,
    normed_ref,
    inverse_ref,
    pad_ref,
    mix_ref,
    west_ref,
    east_ref,
    *sems,
):
    def finish(o, lat, mixed):
        center = mixed - jnp.mean(mixed, axis=1, keepdims=True)
        inverse = lax.rsqrt(jnp.mean(center * center, axis=1, keepdims=True) + eps_norm)
        normal = center * inverse
        normal_ref[o, pl.ds(lat, 16), :] = normal.astype(jnp.bfloat16)
        normed_ref[o, pl.ds(lat, 16), :] = (normal * gain_ref[...]).astype(jnp.bfloat16)
        inverse_ref[o, pl.ds(lat, 16), :] = jnp.broadcast_to(inverse, (16, 128))

    conv_all(mid_ref, kern_ref, pad_ref, mix_ref, west_ref, east_ref, sems, False, finish)


def conv_norm_given_kernel(west_ref, east_ref, *refs):
    conv_norm_kernel(*refs, west_ref, east_ref)


def conv_add_kernel(
    mid_ref, kern_ref, add_ref, out_ref, pad_ref, mix_ref, west_ref, east_ref, *sems
):
    def finish(o, lat, summed):
        total = add_ref[o, pl.ds(lat, 16), :].astype(jnp.float32) + summed
        out_ref[o, pl.ds(lat, 16), :] = total.astype(jnp.bfloat16)

    conv_all(mid_ref, kern_ref, pad_ref, mix_ref, west_ref, east_ref, sems, True, finish)


def conv_scratch(shape):
    lon_rows, lat_cols, hidden = shape
    halves = hidden // 128
    return [
        pltpu.VMEM((halves, lon_rows + 2 * REACH, lat_cols + 16, 128), jnp.float32),
        pltpu.VMEM((halves, lon_rows, 16, 128), jnp.float32),
        pltpu.VMEM((REACH, lat_cols, hidden), jnp.bfloat16),
        pltpu.VMEM((REACH, lat_cols, hidden), jnp.bfloat16),
        pltpu.SemaphoreType.DMA((2,)),
        pltpu.SemaphoreType.DMA((2,)),
    ]


def conv_cost(shape):
    cells = shape[0] * shape[1] * shape[2]
    return pl.CostEstimate(flops=cells * 98, bytes_accessed=cells * 12, transcendentals=0)


def in_vmem(count):
    return [pl.BlockSpec(memory_space=pltpu.VMEM)] * count


def conv_norm(cells, kern, gain, given):
    shape = cells.shape
    return pl.pallas_call(
        conv_norm_given_kernel if given else conv_norm_kernel,
        out_shape=(
            jax.ShapeDtypeStruct(shape, jnp.bfloat16),
            jax.ShapeDtypeStruct(shape, jnp.bfloat16),
            jax.ShapeDtypeStruct(shape[:2] + (128,), jnp.float32),
        ),
        in_specs=in_vmem(5 if given else 3),
        out_specs=tuple(in_vmem(3)),
        scratch_shapes=conv_scratch(shape)[: 2 if given else None],
        cost_estimate=conv_cost(shape),
        compiler_params=pltpu.CompilerParams(vmem_limit_bytes=VMEM_LIMIT)
        if given
        else pltpu.CompilerParams(
            vmem_limit_bytes=VMEM_LIMIT, collective_id=0, has_side_effects=True
        ),
    )(*(edges(cells) if given else ()), cells, kern, gain)


def conv_add(cells, kern, add):
    shape = cells.shape
    return pl.pallas_call(
        conv_add_kernel,
        out_shape=jax.ShapeDtypeStruct(shape, jnp.bfloat16),
        in_specs=in_vmem(3),
        out_specs=pl.BlockSpec(memory_space=pltpu.VMEM),
        scratch_shapes=conv_scratch(shape),
        cost_estimate=conv_cost(shape),
        compiler_params=pltpu.CompilerParams(
            vmem_limit_bytes=VMEM_LIMIT, collective_id=1, has_side_effects=True
        ),
    )(cells, kern, add)


def mlp_kernel(piece, normed_ref, lifted_ref, up_ref, down_ref, block_ref, slope_ref):
    normed = normed_ref[...]
    total = lifted_ref[...].astype(jnp.float32)
    for start in range(0, up_ref.shape[1], piece):
        z = jnp.dot(normed, up_ref[:, start : start + piece], preferred_element_type=jnp.float32)
        square = z * z
        tanh_val = jnp.tanh(z * (root_two_pi + root_two_pi * gelu_coef * square))
        half = 0.5 + 0.5 * tanh_val
        active = (z * half).astype(jnp.bfloat16)
        rest = (1.0 - half).astype(jnp.bfloat16)
        share, arg = half.astype(jnp.bfloat16), z.astype(jnp.bfloat16)
        steep = jnp.bfloat16(6.0 * root_two_pi * gelu_coef)
        bend = arg * (jnp.bfloat16(2.0 * root_two_pi) + steep * (arg * arg))
        slope_ref[:, start : start + piece] = share + share * (rest * bend)
        total = total + jnp.dot(
            active, down_ref[start : start + piece, :], preferred_element_type=jnp.float32
        )
    block_ref[...] = total.astype(jnp.bfloat16)


def mlp(normed, lifted, up_weight, down_weight, rows=512, piece=256):
    amount, hidden = normed.shape
    wide = up_weight.shape[1]
    by_rows = lambda width: pl.BlockSpec((rows, width), lambda r: (r, 0))
    whole = lambda shape: pl.BlockSpec(shape, lambda r: (0, 0))
    return pl.pallas_call(
        functools.partial(mlp_kernel, piece),
        grid=(amount // rows,),
        out_shape=(
            jax.ShapeDtypeStruct((amount, hidden), jnp.bfloat16),
            jax.ShapeDtypeStruct((amount, wide), jnp.bfloat16),
        ),
        in_specs=[by_rows(hidden), by_rows(hidden), whole((hidden, wide)), whole((wide, hidden))],
        out_specs=(by_rows(hidden), by_rows(wide)),
        cost_estimate=pl.CostEstimate(
            flops=4 * amount * hidden * wide,
            bytes_accessed=amount * (wide + 3 * hidden) * 2,
            transcendentals=amount * wide,
        ),
        compiler_params=pltpu.CompilerParams(vmem_limit_bytes=VMEM_LIMIT),
    )(normed, lifted, up_weight, down_weight)


def mlp_back_kernel(
    piece, block_ref, slope_ref, normal_ref, inverse_ref, gain_ref, up_ref, down_ref, out_ref
):
    g_block = block_ref[...]
    across = (((1,), (1,)), ((), ()))
    total = None
    for start in range(0, up_ref.shape[1], piece):
        g_active = lax.dot_general(
            g_block,
            down_ref[start : start + piece, :],
            across,
            preferred_element_type=jnp.float32,
        )
        g_middle = g_active * slope_ref[:, start : start + piece].astype(jnp.float32)
        term = lax.dot_general(
            g_middle.astype(jnp.bfloat16),
            up_ref[:, start : start + piece],
            across,
            preferred_element_type=jnp.float32,
        )
        total = term if total is None else total + term
    g_scaled = total * gain_ref[...]
    normal = normal_ref[...].astype(jnp.float32)
    g_mixed = inverse_ref[:, 0:1] * (
        g_scaled
        - jnp.mean(g_scaled, axis=1, keepdims=True)
        - normal * jnp.mean(g_scaled * normal, axis=1, keepdims=True)
    )
    out_ref[...] = g_mixed.astype(jnp.bfloat16)


def mlp_back(g_block, slope, normal, inverse, gain, up_weight, down_weight, rows=512, piece=256):
    amount, hidden = g_block.shape
    wide = up_weight.shape[1]
    by_rows = lambda width: pl.BlockSpec((rows, width), lambda r: (r, 0))
    whole = lambda shape: pl.BlockSpec(shape, lambda r: (0, 0))
    return pl.pallas_call(
        functools.partial(mlp_back_kernel, piece),
        grid=(amount // rows,),
        out_shape=jax.ShapeDtypeStruct((amount, hidden), jnp.bfloat16),
        in_specs=[
            by_rows(hidden),
            by_rows(wide),
            by_rows(hidden),
            by_rows(128),
            whole((1, hidden)),
            whole((hidden, wide)),
            whole((wide, hidden)),
        ],
        out_specs=by_rows(hidden),
        cost_estimate=pl.CostEstimate(
            flops=4 * amount * hidden * wide,
            bytes_accessed=amount * (2 * wide + 8 * hidden),
            transcendentals=0,
        ),
        compiler_params=pltpu.CompilerParams(vmem_limit_bytes=VMEM_LIMIT),
    )(g_block, slope, normal, inverse, gain, up_weight, down_weight)


def forward_step(state_field, weights, given):
    lift_weight, kern, gain, up_weight, down_weight, out_weight = weights
    channels, lon_rows, lat_cols = state_field.shape
    hidden = lift_weight.shape[1]
    lifted = lax.dot_general(
        state_field.astype(jnp.bfloat16),
        lift_weight,
        (((0,), (0,)), ((), ())),
        preferred_element_type=jnp.float32,
    ).astype(jnp.bfloat16)
    normal, normed, inverse = conv_norm(lifted, kern, gain, given)
    block_out, slope = mlp(
        normed.reshape(-1, hidden), lifted.reshape(-1, hidden), up_weight, down_weight
    )
    change = lax.dot_general(
        out_weight, block_out, (((0,), (1,)), ((), ())), preferred_element_type=jnp.float32
    )
    saved = (normal.reshape(-1, hidden), inverse.reshape(-1, 128), slope)
    return state_field + change.reshape(channels, lon_rows, lat_cols), saved


def backward_step(cotangent, saved, weights):
    lift_weight, kern, gain, up_weight, down_weight, out_weight = weights
    normal, inverse, slope = saved
    channels, lon_rows, lat_cols = cotangent.shape
    hidden = lift_weight.shape[1]
    g_block = lax.dot_general(
        cotangent.astype(jnp.bfloat16),
        out_weight,
        (((0,), (1,)), ((), ())),
        preferred_element_type=jnp.float32,
    ).astype(jnp.bfloat16)
    g_mixed = mlp_back(
        g_block.reshape(-1, hidden), slope, normal, inverse, gain, up_weight, down_weight
    ).reshape(lon_rows, lat_cols, hidden)
    g_lifted = conv_add(g_mixed, kern, g_block)
    g_state = lax.dot_general(
        lift_weight, g_lifted, (((1,), (2,)), ((), ())), preferred_element_type=jnp.float32
    )
    return cotangent + g_state


def tile_ops(cell_ids, point_weights):
    positions = jnp.arange(TILE_CELLS, dtype=jnp.int32)
    return jnp.sum(
        point_weights[..., None] * (cell_ids[..., None] == positions).astype(jnp.float32), axis=2
    )


def to_tiles(state_field):
    channels, lon_rows, lat_cols = state_field.shape
    tile_rows = TILE_CELLS // lon_rows
    split = state_field.reshape(channels, lon_rows, lat_cols // tile_rows, tile_rows)
    return split.transpose(2, 0, 1, 3).reshape(lat_cols // tile_rows, channels, TILE_CELLS)


def from_tiles(tile_sums, lon_rows):
    tile_total, channels, _ = tile_sums.shape
    tile_rows = TILE_CELLS // lon_rows
    split = tile_sums.reshape(tile_total, channels, lon_rows, tile_rows)
    return split.transpose(1, 2, 0, 3).reshape(channels, lon_rows, tile_total * tile_rows)


def slot_selector(owner_ids, band_count, place_count):
    hit = owner_ids[:, None] == jnp.arange(band_count, dtype=jnp.int32)[None, :]
    slots = jnp.arange(owner_ids.shape[0], dtype=jnp.int32)
    earlier = (slots[None, :] < slots[:, None]).astype(jnp.bfloat16)
    before = jnp.dot(earlier, hit.astype(jnp.bfloat16), preferred_element_type=jnp.float32)
    place = jnp.sum(jnp.where(hit, before, 0.0), axis=1).astype(jnp.int32)
    slot_code = owner_ids * place_count + place
    return (
        slot_code[:, None] == jnp.arange(band_count * place_count, dtype=jnp.int32)[None, :]
    ).astype(jnp.bfloat16)


def owners_data(obs_values, obs_precision):
    channels = obs_values.shape[-1]
    widen = ((0, 0), (0, 0), (0, 0), (0, 128 - channels))
    both = jnp.concatenate(
        [jnp.pad(part[:, 0].astype(jnp.bfloat16), widen) for part in (obs_values, obs_precision)],
        axis=3,
    ).transpose(1, 0, 2, 3)
    return lax.all_to_all(both, "lon", split_axis=0, concat_axis=0, tiled=True)


def shards(
    state_start,
    lift_weight,
    conv_kernel,
    norm_gain,
    up_weight,
    down_weight,
    out_weight,
    obs_cells,
    obs_weights,
    tile_counts,
    obs_owner,
    obs_values,
    obs_precision,
):
    hidden = norm_gain.shape[0]
    by_half = lambda taps: jnp.broadcast_to(
        taps.reshape(-1, 1, hidden // 128, 128).transpose(2, 0, 1, 3),
        (hidden // 128, taps.shape[0], 8, 128),
    )
    weights = (
        lift_weight,
        by_half(conv_kernel),
        norm_gain.reshape(1, hidden),
        up_weight,
        down_weight,
        out_weight,
    )
    channels, lon_rows = (state_start.shape[0], state_start.shape[1])
    band_count, place_count = (obs_values.shape[2], obs_values.shape[3])
    tile_total, slot_total = (obs_cells.shape[1], obs_cells.shape[2])
    arrived = owners_data(obs_values, obs_precision)
    operators = [
        tile_ops(obs_cells[moment], obs_weights[moment]).astype(jnp.bfloat16) for moment in range(2)
    ]
    state_one, saved_zero = forward_step(state_start, weights, True)
    state_two, saved_one = forward_step(state_one, weights, False)

    def pulled(moment, state_field):
        selector = slot_selector(obs_owner[moment, :, 0], band_count, place_count)
        chosen = jnp.dot(
            selector,
            arrived[:, moment].reshape(band_count * place_count, -1),
            preferred_element_type=jnp.float32,
        )
        live_slots = (
            (jnp.arange(slot_total, dtype=jnp.int32)[None, :] < tile_counts[moment][:, None])
            .astype(jnp.float32)
            .reshape(-1, 1)
        )
        model_equiv = jnp.einsum(
            "gkc,gsc->gks",
            operators[moment],
            to_tiles(state_field.astype(jnp.bfloat16)),
            preferred_element_type=jnp.float32,
        ).reshape(-1, channels)
        misfit = live_slots * (
            chosen[:, 128 : 128 + channels] * (model_equiv - chosen[:, :channels])
        )
        tile_sums = jnp.einsum(
            "gkc,gks->gsc",
            operators[moment],
            misfit.reshape(tile_total, slot_total, channels).astype(jnp.bfloat16),
            preferred_element_type=jnp.float32,
        )
        return from_tiles(tile_sums, lon_rows)

    carried = backward_step(pulled(1, state_two), saved_one, weights) + pulled(0, state_one)
    return backward_step(carried, saved_zero, weights)


def solution(mesh):
    placed = (
        P("member", "lon", None),
        P(),
        P(),
        P(),
        P(),
        P(),
        P(),
        P("member", "lon", None, None),
        P("member", "lon", None, None),
        P("member", "lon"),
        P("member", "lon", None),
        P("member", "lon", None, None, None),
        P("member", "lon", None, None, None),
    )
    return jax.shard_map(
        shards, mesh=mesh, in_specs=placed, out_specs=P("member", "lon", None), check_vma=False
    )
```
